512 devices in a mesh: dp: 64 (over z, y_lo, core), tensor: 8 (over y_hi, x).
Axes of the slice: x: 4, y: 8 (y_hi: 2, y_lo: 4; y = y_hi * 4 + y_lo), z: 8, core: 2. Of those that a mesh axis runs over, the one named last changes fastest.
Arguments:
- calib_inputs: bfloat16 [49152, 16384], P('dp', 'tensor'), may hold values from -54 to 54, as said below
- weights: bfloat16 [53248, 4096], P(('dp', 'tensor')), may hold values from -6 to 6
- inverse_chol: float32 [256, 4096], P(None, 'dp'), may hold values from -0.3 to 2, as said below
- keep_pattern: int32 [53248, 64], P(('dp', 'tensor')), may hold values from 0 to 5
Outputs:
- pruned_weights: bfloat16 [53248, 4096], P(('dp', 'tensor'))
- gram_panel: float32 [256, 16384], P('dp', 'tensor')
The draws below stay inside these ranges and needn't reach their ends.
Inputs may be any that keep to these rules, and one draw needn't show every extreme that they name: `calib_inputs`: each row (calibration token) and each feature carry their own scale. `inverse_chol`: zero below the diagonal (row j against window column j); the diagonal lies within 0.5 to 2.
All inputs are finite; a program needn't handle non-finite values.
Results may differ from the reference program's by a relative error of at most 0.001.
Values may be sent and summed in bfloat16 or wider, within the bound.
A program may use at most 64 MiB of HBM per device.

```python
import math
import jax
import jax.numpy as jnp
import numpy as np
from jax import lax

D = 16384
ROWS_DEV = 104
FF = 53248
DW = 4096
PANEL = 128
GROUPS = 64
TOKENS = 49152


def draw_calib_inputs(key, part):
    key = jax.random.fold_in(key, 11)
    key_list = jax.random.split(key, 3)
    low_log = math.log(0.3)
    high_log = math.log(3.0)
    row_scale = jnp.exp(jax.random.uniform(key_list[1], (TOKENS, 1), jnp.float32, low_log, high_log))
    col_scale = jnp.exp(jax.random.uniform(key_list[2], (1, D), jnp.float32, low_log, high_log))
    base_values = jnp.clip(jax.random.normal(key_list[0], (TOKENS, D), jnp.float32), -6.0, 6.0)
    return (base_values * row_scale * col_scale).astype(jnp.bfloat16)


def draw_inverse_chol(key, part):
    key = jax.random.fold_in(key, 23)
    key_list = jax.random.split(key, 2)
    row_count = 2 * PANEL
    row_id = jnp.arange(row_count, dtype=jnp.int32)[:, None]
    col_id = jnp.arange(DW, dtype=jnp.int32)[None, :]
    diagonal = jnp.exp(jax.random.uniform(key_list[0], (row_count, 1), jnp.float32, math.log(0.5), math.log(2.0)))
    off_values = jnp.clip(0.06 * jax.random.normal(key_list[1], (row_count, DW), jnp.float32), -0.3, 0.3)
    upper_part = jnp.where(col_id > row_id, off_values, jnp.float32(0.0))
    return jnp.where(col_id == row_id, diagonal, upper_part).astype(jnp.float32)


def plant(values, stream_key, least, largest):
    spot = [jax.random.randint(jax.random.fold_in(stream_key, axis), (), 0, length) for axis, length in enumerate(values.shape)]
    main_axis = values.shape.index(max(values.shape))
    neighbour = spot[:main_axis] + [(spot[main_axis] + 1) % values.shape[main_axis]] + spot[main_axis + 1:]
    return values.at[tuple(spot)].set(least).at[tuple(neighbour)].set(largest)


def levels(own_key, dims, shards, low, high):
    level = 1.0
    for axis_at, shards_of in shards:
        steps = jax.random.uniform(jax.random.fold_in(jax.random.fold_in(own_key, 6), axis_at), (shards_of,), jnp.float32, low / len(shards), high / len(shards))
        level = level * jnp.repeat(jnp.exp(steps), dims[axis_at] // shards_of).reshape((-1,) + (1,) * (len(dims) - 1 - axis_at))
    return level


def noise(stream_key, dims, deviation, reach, cuts=(), kind=jnp.bfloat16):
    result = jax.random.normal(stream_key, dims, jnp.float32) * deviation
    if len(cuts) > 0:
        result = levels(stream_key, dims, cuts, -0.22, 0.18) * result
    return jnp.clip(result, min=-reach, max=reach).astype(kind)


def setup_inputs(seed: int = 0) -> dict:
    streams_of = jax.random.split(jax.random.key(seed), 5)
    return {
        "calib_inputs": draw_calib_inputs(jax.random.fold_in(streams_of[4], 71), 0),
        "weights": noise(streams_of[1], (FF, DW), 1.0, 6.0, ((0, 512),)),
        "inverse_chol": draw_inverse_chol(jax.random.fold_in(streams_of[4], 71), 0),
        "keep_pattern": plant(jax.random.randint(streams_of[3], (FF, GROUPS), 0, 6), jax.random.fold_in(streams_of[3], 1), 0, 5).astype(jnp.int32),
    }


def keep_columns(pattern_rows, panel_width):
    first_pos = jnp.array(np.array([0, 0, 0, 1, 1, 2]), dtype=jnp.int32)
    second_pos = jnp.array(np.array([1, 2, 3, 2, 3, 3]), dtype=jnp.int32)
    pattern_cols = jnp.repeat(pattern_rows, 4, axis=1)
    position = jnp.arange(panel_width, dtype=jnp.int32) % 4
    chosen = pattern_cols[:, :, None] == jnp.arange(6, dtype=jnp.int32)[None, None, :]
    first_sel = jnp.sum(jnp.where(chosen, first_pos[None, None, :], 0), axis=-1)
    second_sel = jnp.sum(jnp.where(chosen, second_pos[None, None, :], 0), axis=-1)
    hit = (position[None, :] == first_sel) | (position[None, :] == second_sel)
    return jnp.where(hit, 1.0, 0.0).astype(jnp.float32)


def sweep_step(column_at, carry, keep_cols, head_block, col_index):
    panel_cols, errors = carry
    column = lax.dynamic_slice_in_dim(panel_cols, column_at, 1, 1)[:, 0]
    keep_col = lax.dynamic_slice_in_dim(keep_cols, column_at, 1, 1)[:, 0]
    pruned_col = column * keep_col
    chol_row = lax.dynamic_slice_in_dim(head_block, column_at, 1, 0)[0]
    pivot_value = lax.dynamic_slice_in_dim(chol_row, column_at, 1, 0)[0]
    error_col = (column - pruned_col) / pivot_value
    row_after = jnp.where(col_index > column_at, chol_row, jnp.float32(0.0))
    panel_cols = panel_cols - error_col[:, None] * row_after[None, :]
    select = (col_index == column_at)[None, :]
    panel_cols = jnp.where(select, pruned_col[:, None], panel_cols)
    errors = jnp.where(select, error_col[:, None], errors)
    return panel_cols, errors


def prune_rows(weight_rows, pattern_rows, inverse_chol):
    panel_width = inverse_chol.shape[0]
    weight_f32 = weight_rows.astype(jnp.float32)
    keep_cols = keep_columns(pattern_rows, panel_width)
    head_block = inverse_chol[:, :panel_width]
    col_index = jnp.arange(panel_width, dtype=jnp.int32)

    def advance(column_at, carry):
        return sweep_step(column_at, carry, keep_cols, head_block, col_index)

    start_state = (weight_f32[:, :panel_width], jnp.zeros_like(weight_f32[:, :panel_width]))
    panel_cols, errors = lax.fori_loop(jnp.int32(0), jnp.int32(panel_width), advance, start_state)
    tail_cols = weight_f32[:, panel_width:] - jnp.dot(errors, inverse_chol[:, panel_width:], precision=lax.Precision.HIGHEST, preferred_element_type=jnp.float32)
    return jnp.concatenate([panel_cols, tail_cols], axis=1).astype(jnp.bfloat16)


def reference(calib_inputs, weights, inverse_chol, keep_pattern):
    panel_width = 2 * PANEL
    window_start = D - DW
    panel_inputs = calib_inputs[:, window_start:window_start + panel_width]
    gram_rows = lax.dot_general(panel_inputs, calib_inputs, (((0,), (0,)), ((), ())), preferred_element_type=jnp.float32)
    gram_panel = gram_rows * (2.0 / TOKENS)
    weight_blocks = weights.reshape(-1, ROWS_DEV, DW)
    pattern_blocks = keep_pattern.reshape(-1, ROWS_DEV, GROUPS)

    def one_block(pair_rows):
        return prune_rows(pair_rows[0], pair_rows[1], inverse_chol)

    pruned_blocks = lax.map(one_block, (weight_blocks, pattern_blocks))
    pruned_weights = pruned_blocks.reshape(FF, DW)
    return pruned_weights, gram_panel
```

```python
import jax
import jax.numpy as jnp
from jax import lax
from jax.experimental import pallas as pl
from jax.experimental.pallas import tpu as pltpu
from jax.sharding import PartitionSpec as P

MESH = pl.DeviceIdType.MESH
NZ, NY, NC, NH, NX = 8, 4, 2, 2, 4
PANEL_W = 256
WINDOW = 4096
ROWS = 104
LANES = 128
FEAT = 2048
TOK = 768
QTOK = TOK // NX
PART = PANEL_W // (NX * NC)
OWNER_X, OWNER_H = 2, 1
BLOCK = 32
CODE_MAX = 32767.0
CHOL_MAX = 2.0
SUM_MAX = 32000.0
F32 = jnp.float32
BF16 = jnp.bfloat16
HIGHEST = lax.Precision.HIGHEST


def contract(a, b, da, db, precision=None):
    return lax.dot_general(
        a, b, (((da,), (db,)), ((), ())), precision=precision, preferred_element_type=F32
    )


def identity(n, dtype):
    rows = lax.broadcasted_iota(jnp.int32, (n, n), 0)
    cols = lax.broadcasted_iota(jnp.int32, (n, n), 1)
    return jnp.where(rows == cols, 1.0, 0.0).astype(dtype)


def panel_order():
    rows = lax.broadcasted_iota(jnp.int32, (PANEL_W, PANEL_W), 0)
    cols = lax.broadcasted_iota(jnp.int32, (PANEL_W, PANEL_W), 1)
    core, rest = rows // 128, rows % 128
    feature = (rest // 4) * 8 + core * 4 + rest % 4
    return jnp.where(feature == cols, 1.0, 0.0).astype(BF16)


def encode_chol(value):
    root = jnp.sqrt(jnp.minimum(jnp.abs(value) * (1.0 / CHOL_MAX), 1.0)) * CODE_MAX
    code = jnp.round(jnp.where(value < 0.0, -root, root))
    return code.astype(jnp.int32).astype(jnp.int16)


def decode_chol(code):
    value = code.astype(jnp.int32).astype(F32)
    return value * jnp.abs(value) * (CHOL_MAX / (CODE_MAX * CODE_MAX))


def kernel(
    calib, weights, inverse, pattern,
    pruned, gram,
    xv, pv, wv, kv, iv, ipeer, qv, hv, gv, gpeer, msend, mrecv, ysend, yrecv,
    wpad, kpad, dg, ct, av, et, eh, el, pt,
    lsem, isem, s1s, s1r, s2s, s2r, qzs, qzr, qys, qyr, qxs, qxr, hzs, hzr, hys, hyr, hxs, hxr,
    ccs, ccr, gcs, gcr, rzs, rzr, rys, ryr,
):
    d = lax.axis_index("dp")
    t = lax.axis_index("tensor")
    z, y, c = d // (NY * NC), (d // NC) % NY, d % NC
    h, x = t // NX, t % NX
    owner = (h == OWNER_H) & (x == OWNER_X)

    def at(z=z, y=y, c=c, h=h, x=x):
        return ((z * NY + y) * NC + c, h * NX + x)

    def remote(src, dst, send, recv, where):
        return pltpu.make_async_remote_copy(
            src_ref=src, dst_ref=dst, send_sem=send, recv_sem=recv,
            device_id=where, device_id_type=MESH,
        )

    def zp(k):
        return lax.rem(z + k, NZ)

    def yp(k):
        return lax.rem(y + k, NY)

    def xp(k):
        return lax.rem(x + k, NX)

    load_i = pltpu.make_async_copy(inverse, iv, lsem.at[0])
    load_x = pltpu.make_async_copy(calib, xv, lsem.at[1])
    load_w = pltpu.make_async_copy(weights, wv, lsem.at[2])
    load_k = pltpu.make_async_copy(pattern, kv, lsem.at[3])
    load_p = pltpu.make_async_copy(calib.at[:, pl.ds(0, PANEL_W)], pv, lsem.at[4])
    load_i.start()
    pl.when(owner)(load_p.start)
    load_x.start()
    load_w.start()
    load_k.start()

    barrier = pltpu.get_barrier_semaphore()
    partners = [at(c=1 - c)]
    partners += [at(z=zp(k)) for k in range(1, NZ)]
    partners += [at(y=yp(k)) for k in range(1, NY)]
    partners += [at(x=xp(k)) for k in range(1, NX)]
    partners += [at(h=1 - h, x=xp(k)) for k in range(NX)]
    for partner in partners:
        pl.semaphore_signal(barrier, inc=1, device_id=partner, device_id_type=MESH)
    pl.semaphore_wait(barrier, len(partners))

    scatter = []
    for k in range(1, NH * NX):
        td = lax.rem(t + k, NH * NX)
        rows = pl.ds(pl.multiple_of(lax.rem(td, NX) * QTOK, QTOK), QTOK)
        scatter.append(
            remote(calib.at[rows, pl.ds(0, PANEL_W)], pv.at[rows], s1s.at[k - 1], s1r.at[0], (d, td))
        )

    @pl.when(owner)
    def _():
        for copy in scatter:
            copy.start()

    load_i.wait()
    pair = remote(iv, ipeer, isem.at[0], isem.at[1], at(c=1 - c))
    pair.start()

    my_quarter = pl.ds(pl.multiple_of(x * QTOK, QTOK), QTOK)
    part_at = pl.multiple_of(c * 128 + x * PART, PART)
    part = pl.ds(part_at, PART)
    half = pl.ds(pl.multiple_of(c * 128, 128), 128)

    pair.wait_recv()
    mine = iv[part, :]
    peers = ipeer[part, :]
    even = jnp.full(mine.shape, c, jnp.int32) == 0
    block = jnp.concatenate([jnp.where(even, mine, peers), jnp.where(even, peers, mine)], axis=1)
    my_cols = pl.ds(pl.multiple_of(z * 128, 128), 128)
    qv[y, part, my_cols] = encode_chol(block)
    head_chip = (z == 0) & (y < 2)
    head_line = y < 2
    hy = jnp.minimum(y, 1)

    @pl.when(head_chip)
    def _():
        hv[hy, part, :] = block

    q_z = [
        remote(qv.at[y, part, my_cols], qv.at[y, part, my_cols], qzs.at[k - 1], qzr.at[k - 1], at(z=zp(k)))
        for k in range(1, NZ)
    ]
    h_z = [
        remote(hv.at[hy, part], hv.at[hy, part], hzs.at[k - 1], hzr.at[0], at(z=zp(k)))
        for k in range(1, NZ)
    ]

    @pl.when(head_chip)
    def _():
        for copy in h_z:
            copy.start()

    for copy in q_z:
        copy.start()

    @pl.when(owner)
    def _():
        load_p.wait()

    @pl.when(jnp.logical_not(owner))
    def _():
        remote(pv.at[my_quarter], pv.at[my_quarter], s1s.at[0], s1r.at[0], at(c=1 - c)).wait_recv()

    share = []
    for k in range(1, NX):
        to_owner = (h == OWNER_H) & (xp(k) == OWNER_X)
        copy = remote(pv.at[my_quarter], pv.at[my_quarter], s2s.at[k - 1], s2r.at[k - 1], at(x=xp(k)))
        pl.when(jnp.logical_not(to_owner))(copy.start)
        share.append((copy, to_owner))

    for k in range(1, NZ):
        cols = pl.ds(pl.multiple_of(zp(NZ - k) * 128, 128), 128)
        remote(qv.at[y, part, cols], qv.at[y, part, cols], qzs.at[k - 1], qzr.at[k - 1], at(z=zp(k))).wait_recv()

    @pl.when(head_line & (z > 0))
    def _():
        h_z[0].wait_recv()

    h_y = [
        remote(hv.at[hy, part], hv.at[hy, part], hys.at[k - 1], hyr.at[k - 1], at(y=yp(k)))
        for k in range(1, NY)
    ]

    @pl.when(head_line)
    def _():
        for copy in h_y:
            copy.start()

    q_y = [
        remote(qv.at[y, part], qv.at[y, part], qys.at[k - 1], qyr.at[k - 1], at(y=yp(k)))
        for k in range(1, NY)
    ]
    for copy in q_y:
        copy.start()

    for k in range(1, NX):
        rows = pl.ds(pl.multiple_of(xp(NX - k) * QTOK, QTOK), QTOK)

        @pl.when(jnp.logical_not(owner))
        def _():
            remote(pv.at[rows], pv.at[rows], s2s.at[k - 1], s2r.at[k - 1], at(x=xp(k))).wait_recv()

    load_x.wait()
    pt[...] = contract(panel_order(), pv[...], 1, 1).astype(BF16)
    g_c = []
    for tile in range(4):
        cols = slice(tile * 512, tile * 512 + 512)
        gv[tile] = contract(pt[...], xv[:, cols], 1, 0).reshape(2, 128, 512)
        copy = remote(gv.at[tile, 1 - c], gpeer.at[tile], gcs.at[tile], gcr.at[tile], at(c=1 - c))
        copy.start()
        g_c.append(copy)

    for k in range(1, NY):
        yo = yp(NY - k)
        remote(qv.at[yo, part], qv.at[yo, part], qys.at[k - 1], qyr.at[k - 1], at(y=yp(k))).wait_recv()
        ho = jnp.minimum(yo, 1)

        @pl.when(yo < 2)
        def _():
            remote(hv.at[ho, part], hv.at[ho, part], hys.at[k - 1], hyr.at[k - 1], at(y=yp(k))).wait_recv()

    h_x = [remote(hv.at[:, part], hv.at[:, part], hxs.at[k - 1], hxr.at[k - 1], at(x=xp(k))) for k in range(1, NX)]
    q_x = [remote(qv.at[:, part], qv.at[:, part], qxs.at[k - 1], qxr.at[k - 1], at(x=xp(k))) for k in range(1, NX)]
    for copy in h_x + q_x:
        copy.start()

    for copy in g_c:
        copy.wait_recv()

    def pack(k, carry):
        zd = lax.rem(z + k, NZ)
        rows = pl.ds(pl.multiple_of(zd * 16, 16), 16)
        parts = [gv[tile, c, rows, :] + gpeer[tile, rows, :] for tile in range(4)]
        for tile in range(4):
            gpeer[tile, rows, :] = parts[tile]
        tiles = [p[:, 128 * i : 128 * i + 128] for p in parts for i in range(4)]
        most = jnp.abs(tiles[0])
        for value in tiles[1:]:
            most = jnp.maximum(most, jnp.abs(value))
        most = jnp.max(most, axis=0, keepdims=True)
        power = jnp.ceil(jnp.log2(jnp.maximum(most, 1e-30)))
        up = jnp.exp2(-power) * SUM_MAX
        for i, value in enumerate(tiles):
            msend[zd, i] = jnp.round(value * up).astype(jnp.int32).astype(jnp.int16)
        msend[zd, 16] = jnp.broadcast_to(power, (16, 128)).astype(jnp.int32).astype(jnp.int16)
        return carry

    lax.fori_loop(0, NZ, pack, 0)
    r_z = [
        remote(msend.at[zp(k)], mrecv.at[k - 1], rzs.at[k - 1], rzr.at[k - 1], at(z=zp(k)))
        for k in (4, 3, 5, 2, 6, 1, 7)
    ]
    for copy in r_z:
        copy.start()

    load_w.wait()
    load_k.wait()
    wpad[...] = jnp.zeros_like(wpad)
    wpad[0:ROWS, :] = wv[:, 0:PANEL_W].astype(F32)
    kpad[...] = jnp.zeros_like(kpad)
    kpad[0:ROWS, 0:64] = kv[...].astype(F32)
    ct[...] = contract(identity(PANEL_W, BF16), wpad[...].astype(BF16), 1, 1)
    col_id = lax.broadcasted_iota(jnp.int32, (PANEL_W, LANES), 0)
    group_id = lax.broadcasted_iota(jnp.int32, (PANEL_W, LANES), 1)
    repeat = jnp.where(col_id // 4 == group_id, 1.0, 0.0).astype(BF16)
    choice = contract(repeat, kpad[...].astype(BF16), 1, 1).astype(jnp.int32)
    place = col_id % 4
    drop = (
        ((place == 0) & (choice >= 3))
        | ((place == 1) & ((choice == 1) | (choice == 2) | (choice == 5)))
        | ((place == 2) & ((choice == 0) | (choice == 2) | (choice == 4)))
        | ((place == 3) & ((choice == 0) | (choice == 1) | (choice == 3)))
    )

    for k in range(1, NX):
        rows = pl.ds(pl.multiple_of(c * 128 + xp(NX - k) * PART, PART), PART)
        remote(hv.at[:, rows], hv.at[:, rows], hxs.at[k - 1], hxr.at[k - 1], at(x=xp(k))).wait_recv()
    other = pl.ds(pl.multiple_of((1 - c) * 128, 128), 128)
    h_c = remote(hv.at[:, half], hv.at[:, half], ccs.at[0], ccr.at[0], at(c=1 - c))
    h_c.start()
    remote(hv.at[:, other], hv.at[:, other], ccs.at[0], ccr.at[0], at(c=1 - c)).wait_recv()

    head = jnp.concatenate([hv[0], hv[1]], axis=1)
    row_id = lax.broadcasted_iota(jnp.int32, (PANEL_W, PANEL_W), 0)
    lane_id = lax.broadcasted_iota(jnp.int32, (PANEL_W, PANEL_W), 1)
    pivot = jnp.sum(jnp.where(row_id == lane_id, head, 0.0), axis=1, keepdims=True)
    av[...] = jnp.where(drop, jnp.broadcast_to(1.0 / pivot, (PANEL_W, LANES)), 0.0)
    upper = jnp.where(lane_id > row_id, head, 0.0).T
    for b in range(PANEL_W // BLOCK):
        at_b = b * BLOCK
        dg[b, :, 0:BLOCK] = upper[at_b : at_b + BLOCK, at_b : at_b + BLOCK]

    def sweep(b, carry):
        rows = pl.ds(pl.multiple_of(b * BLOCK, BLOCK), BLOCK)
        factor = av[rows, :]
        corner = dg[b]
        now = ct[rows, :]
        cols = [now[8 * v : 8 * v + 8, :] for v in range(BLOCK // 8)]
        for j in range(BLOCK):
            v0 = j // 8
            err = cols[v0][j % 8 : j % 8 + 1, :] * factor[j : j + 1, :]
            for v in range(v0, BLOCK // 8):
                cols[v] = cols[v] - corner[8 * v : 8 * v + 8, j : j + 1] * err
        done = jnp.concatenate(cols, axis=0)
        errors = done * factor
        et[rows, :] = errors
        chol_rows = jnp.concatenate([hv[0, rows, :], hv[1, rows, :]], axis=1)
        update = contract(chol_rows, errors, 0, 0, HIGHEST)
        later = col_id >= (b + 1) * BLOCK
        ct[...] = ct[...] - jnp.where(later, update, 0.0)
        ct[rows, :] = done
        return carry

    lax.fori_loop(0, PANEL_W // BLOCK, sweep, 0)
    kept = jnp.where(drop, 0.0, ct[...]).astype(BF16)
    eye = identity(PANEL_W, BF16)
    kept_rows = contract(kept, eye, 0, 0)
    errors = et[...]
    errors_hi = errors.astype(BF16)
    errors_lo = (errors - errors_hi.astype(F32)).astype(BF16)
    eh[...] = contract(errors_hi, eye, 0, 0).astype(BF16)
    el[...] = contract(errors_lo, eye, 0, 0).astype(BF16)

    for k in range(1, NX):
        rows = pl.ds(pl.multiple_of(c * 128 + xp(NX - k) * PART, PART), PART)
        remote(qv.at[:, rows], qv.at[:, rows], qxs.at[k - 1], qxr.at[k - 1], at(x=xp(k))).wait_recv()
    q_c = remote(qv.at[:, half], qv.at[:, half], ccs.at[1], ccr.at[1], at(c=1 - c))
    q_c.start()

    for k in range(1, NZ):
        remote(msend.at[zp(k)], mrecv.at[k - 1], rzs.at[k - 1], rzr.at[k - 1], at(z=zp(k))).wait_recv()
    own = pl.ds(pl.multiple_of(z * 16, 16), 16)

    for tile in range(4):
        def collect(k, total):
            down = jnp.exp2(mrecv[k, 16].astype(jnp.int32).astype(F32)) * (1.0 / SUM_MAX)
            pieces = [
                mrecv[k, tile * 4 + i].astype(jnp.int32).astype(F32) * down for i in range(4)
            ]
            return total + jnp.concatenate(pieces, axis=1)

        gpeer[tile, own, :] = lax.fori_loop(0, NZ - 1, collect, gpeer[tile, own, :])
    for tile in range(4):
        summed = gpeer[tile, own, :]
        for yd in range(NY):
            ysend[yd, tile * 4 : tile * 4 + 4, :] = summed[yd * 4 : yd * 4 + 4, :]
    r_y = [
        remote(ysend.at[yp(k)], yrecv.at[k - 1], rys.at[k - 1], ryr.at[k - 1], at(y=yp(k)))
        for k in range(1, NY)
    ]
    for copy in r_y:
        copy.start()

    remote(qv.at[:, other], qv.at[:, other], ccs.at[1], ccr.at[1], at(c=1 - c)).wait_recv()

    def tail(step, carry):
        yq, zq = step // 4, (step % 4) * 2
        code = qv[yq, :, pl.ds(pl.multiple_of(zq * 128, 256), 256)]
        chol = decode_chol(code)
        chol_hi = chol.astype(BF16)
        chol_lo = (chol - chol_hi.astype(F32)).astype(BF16)
        update = contract(eh[...], chol_hi, 1, 0) + (
            contract(eh[...], chol_lo, 1, 0) + contract(el[...], chol_hi, 1, 0)
        )
        for i in range(2):
            cols = pl.ds(pl.multiple_of(((zq + i) * 4 + yq) * 128, 128), 128)
            pruned[:, cols] = (
                wv[:, cols].astype(F32) - update[0:ROWS, 128 * i : 128 * i + 128]
            ).astype(BF16)
        return carry

    lax.fori_loop(0, 16, tail, 0)
    pruned[:, 0:PANEL_W] = kept_rows[0:ROWS, :].astype(BF16)

    for copy in r_y:
        copy.wait_recv()
    total = ysend[y] + yrecv[0] + yrecv[1] + yrecv[2]
    total = total * (2.0 / (TOK * NZ * NY * NC))
    for tile in range(4):
        gram[:, tile * 512 : tile * 512 + 512] = total[tile * 4 : tile * 4 + 4, :]

    @pl.when(owner)
    def _():
        for copy in scatter:
            copy.wait_send()

    @pl.when(head_chip)
    def _():
        for copy in h_z:
            copy.wait_send()

    @pl.when(head_line)
    def _():
        for copy in h_y:
            copy.wait_send()

    for copy, to_owner in share:
        pl.when(jnp.logical_not(to_owner))(copy.wait_send)
    for copy in [pair] + q_z + q_y + h_x + q_x + g_c + r_z + [h_c, q_c] + r_y:
        copy.wait_send()


def shards(calib_inputs, weights, inverse_chol, keep_pattern):
    dma = pltpu.SemaphoreType.DMA
    vmem = pltpu.VMEM
    scratch = [
        vmem((TOK, FEAT), BF16),
        vmem((TOK, PANEL_W), BF16),
        vmem((ROWS, WINDOW), BF16),
        vmem((ROWS, 64), jnp.int32),
        vmem((PANEL_W, 64), F32),
        vmem((PANEL_W, 64), F32),
        vmem((NY, PANEL_W, NZ * 128), jnp.int16),
        vmem((2, PANEL_W, 128), F32),
        vmem((4, 2, 128, 512), F32),
        vmem((4, 128, 512), F32),
        vmem((NZ, 17, 16, 128), jnp.int16),
        vmem((NZ - 1, 17, 16, 128), jnp.int16),
        vmem((NY, 16, 512), F32),
        vmem((NY - 1, 16, 512), F32),
        vmem((LANES, PANEL_W), F32),
        vmem((LANES, LANES), F32),
        vmem((PANEL_W // BLOCK, BLOCK, 128), F32),
        vmem((PANEL_W, LANES), F32),
        vmem((PANEL_W, LANES), F32),
        vmem((PANEL_W, LANES), F32),
        vmem((LANES, PANEL_W), BF16),
        vmem((LANES, PANEL_W), BF16),
        vmem((PANEL_W, TOK), BF16),
    ]
    sems = [5, 2, 7, 1, 3, 3, 7, 7, 3, 3, 3, 3, 7, 1, 3, 3, 3, 3, 2, 2, 4, 4, 7, 7, 3, 3]
    scratch += [dma((n,)) for n in sems]
    anywhere = pl.BlockSpec(memory_space=pl.ANY)
    inside = pl.BlockSpec(memory_space=pltpu.VMEM)
    return pl.pallas_call(
        kernel,
        out_shape=(
            jax.ShapeDtypeStruct((ROWS, WINDOW), BF16),
            jax.ShapeDtypeStruct((PANEL_W // (NZ * NY * NC), FEAT), F32),
        ),
        in_specs=[anywhere] * 4,
        out_specs=(inside, inside),
        scratch_shapes=scratch,
        compiler_params=pltpu.CompilerParams(
            collective_id=0, has_side_effects=True, vmem_limit_bytes=40 * 2**20
        ),
        cost_estimate=pl.CostEstimate(flops=2 * 10**9, bytes_accessed=8 * 10**6, transcendentals=0),
    )(calib_inputs, weights, inverse_chol, keep_pattern)


def solution(mesh):
    placed = (
        P("dp", "tensor"),
        P(("dp", "tensor"), None),
        P(None, "dp"),
        P(("dp", "tensor"), None),
    )
    return jax.shard_map(
        shards,
        mesh=mesh,
        in_specs=placed,
        out_specs=(P(("dp", "tensor"), None), P("dp", "tensor")),
        check_vma=False,
    )
```

```python
import jax
import jax.numpy as jnp
from jax import lax
from jax.experimental import pallas as pl
from jax.experimental.pallas import tpu as pltpu
from jax.sharding import PartitionSpec as P

MESH = pl.DeviceIdType.MESH
NZ, NY, NC, NH, NX = 8, 4, 2, 2, 4
PANEL_W = 256
WINDOW = 4096
ROWS = 104
LANES = 128
FEAT = 2048
TOK = 768
QTOK = TOK // NX
PART = PANEL_W // (NX * NC)
OWNER_X, OWNER_H = 2, 1
BLOCK = 32
CODE_MAX = 32767.0
CHOL_MAX = 2.0
SUM_MAX = 32000.0
F32 = jnp.float32
BF16 = jnp.bfloat16
HIGHEST = lax.Precision.HIGHEST


def contract(a, b, da, db, precision=None):
    return lax.dot_general(
        a, b, (((da,), (db,)), ((), ())), precision=precision, preferred_element_type=F32
    )


def identity(n, dtype):
    rows = lax.broadcasted_iota(jnp.int32, (n, n), 0)
    cols = lax.broadcasted_iota(jnp.int32, (n, n), 1)
    return jnp.where(rows == cols, 1.0, 0.0).astype(dtype)


def panel_order():
    rows = lax.broadcasted_iota(jnp.int32, (PANEL_W, PANEL_W), 0)
    cols = lax.broadcasted_iota(jnp.int32, (PANEL_W, PANEL_W), 1)
    core, rest = rows // 128, rows % 128
    feature = (rest // 4) * 8 + core * 4 + rest % 4
    return jnp.where(feature == cols, 1.0, 0.0).astype(BF16)


def encode_chol(value):
    root = jnp.sqrt(jnp.minimum(jnp.abs(value) * (1.0 / CHOL_MAX), 1.0)) * CODE_MAX
    code = jnp.round(jnp.where(value < 0.0, -root, root))
    return code.astype(jnp.int32).astype(jnp.int16)


def decode_chol(code):
    value = code.astype(jnp.int32).astype(F32)
    return value * jnp.abs(value) * (CHOL_MAX / (CODE_MAX * CODE_MAX))


ORDER = (0, 1, 7, 2, 6, 3, 5, 4)


def kernel(
    calib, weights, inverse, pattern,
    pruned, gram,
    xv, pv, wv, kv, iv, ipeer, blk, qv, hv, gv, msend, mrecv, ysend, yrecv,
    wpad, kpad, dg, ct, av, et, eh, el, po, pt,
    lsem, isem, s1s, s1r, hcs, hcr, s2s, s2r,
    qys, qyr, qzs, qzr, qxs, qxr, qcs, qcr, hys, hyr, hzs, hzr, hxs, hxr, hs, hr,
    xcs, xcr, rzs, rzr, rys, ryr,
):
    d = lax.axis_index("dp")
    t = lax.axis_index("tensor")
    z, y, c = d // (NY * NC), (d // NC) % NY, d % NC
    h, x = t // NX, t % NX
    owner = (h == OWNER_H) & (x == OWNER_X)
    not_owner = jnp.logical_not(owner)
    owner_side = h == OWNER_H

    def at(z=z, y=y, c=c, h=h, x=x):
        return ((z * NY + y) * NC + c, h * NX + x)

    def remote(src, dst, send, recv, where):
        return pltpu.make_async_remote_copy(
            src_ref=src, dst_ref=dst, send_sem=send, recv_sem=recv,
            device_id=where, device_id_type=MESH,
        )

    def zp(k):
        return lax.rem(z + k + NZ, NZ)

    def yp(k):
        return lax.rem(y + k, NY)

    def xp(k):
        return lax.rem(x + k, NX)

    def span(start, size):
        return pl.ds(pl.multiple_of(start, size), size)

    load_i = pltpu.make_async_copy(inverse, iv, lsem.at[0])
    load_x = pltpu.make_async_copy(calib, xv.at[c], lsem.at[1])
    load_w = pltpu.make_async_copy(weights, wv, lsem.at[2])
    load_k = pltpu.make_async_copy(pattern, kv, lsem.at[3])
    load_p = pltpu.make_async_copy(calib.at[:, pl.ds(0, PANEL_W)], pv, lsem.at[4])
    pl.when(owner)(load_p.start)
    load_i.start()
    load_x.start()
    load_w.start()
    load_k.start()

    barrier = pltpu.get_barrier_semaphore()
    partners = [at(c=1 - c), at(h=1 - h), at(h=1 - h, c=1 - c)]
    partners += [at(x=xp(k), c=1 - c) for k in range(1, NX)]
    partners += [at(z=zp(k)) for k in range(1, NZ)]
    partners += [at(y=yp(k)) for k in range(1, NY)]
    partners += [at(x=xp(k)) for k in range(1, NX)]
    for partner in partners:
        pl.semaphore_signal(barrier, inc=1, device_id=partner, device_id_type=MESH)

    @pl.when(owner)
    def _():
        load_p.wait()
        po[...] = contract(panel_order(), pv[...], 1, 1).astype(BF16)
        pt[c] = po[span(c * 128, 128), :]

    load_i.wait()
    pl.semaphore_wait(barrier, len(partners))

    def ordered(a, xo):
        return po.at[span(a * 128 + xo * PART, PART)]

    def piece(s, xo):
        return pt.at[s, span(xo * PART, PART)]

    def scatter(a, k):
        return remote(ordered(a, xp(k)), piece(c, xp(k)), s1s.at[a * 3 + k - 1], s1r.at[c], at(x=xp(k), c=a))

    def scattered(s):
        return remote(piece(s, x), piece(s, x), s1s.at[s], s1r.at[s], at(x=xp(1)))

    def across_owner(a):
        return remote(ordered(a, x), piece(c, x), hcs.at[a], hcr.at[c], at(h=1 - h, c=a))

    def across(s):
        return remote(piece(s, x), piece(s, x), hcs.at[s], hcr.at[s], at(h=1 - h))

    def share_owner(a, k):
        sem = s2r.at[c * 3 + k - 1]
        return remote(ordered(a, x), piece(c, x), s2s.at[a * 3 + k - 1], sem, at(x=xp(k), c=a))

    def share(s, k):
        return remote(piece(s, x), piece(s, x), s2s.at[s * 3 + k - 1], s2r.at[s * 3 + k - 1], at(x=xp(k)))

    def shared(s, k):
        src = piece(s, xp(NX - k))
        return remote(src, src, s2s.at[s * 3 + k - 1], s2r.at[s * 3 + k - 1], at(x=xp(k)))

    swap_p = remote(po.at[span((1 - c) * 128, 128)], pt.at[c], xcs.at[0], xcr.at[0], at(c=1 - c))
    swap_x = remote(xv.at[c], xv.at[c], xcs.at[1], xcr.at[1], at(c=1 - c))

    def to_owner(k):
        return owner_side & (xp(k) == OWNER_X)

    def start_share(a):
        for k in (2, 1, 3):
            pl.when(jnp.logical_not(to_owner(k)))(share(a, k).start)

    pair = remote(iv, ipeer, isem.at[0], isem.at[1], at(c=1 - c))
    pair.start()

    @pl.when(owner)
    def _():
        for a in range(2):
            for k in (2, 1, 3):
                scatter(a, k).start()
            across_owner(a).start()
        swap_p.start()

    load_x.wait()
    swap_x.start()

    part = span(c * 128 + x * PART, PART)
    half = span(c * 128, 128)
    other = span((1 - c) * 128, 128)
    head_chip = (z == 0) & (y < 2)
    hcols = span(jnp.minimum(y, 1) * 128, 128)

    pair.wait_recv()
    even = jnp.full(iv.shape, c, jnp.int32) == 0
    blk[...] = jnp.concatenate(
        [jnp.where(even, iv[...], ipeer[...]), jnp.where(even, ipeer[...], iv[...])], axis=0
    ).T

    @pl.when(head_chip)
    def _():
        hv[part, hcols] = blk[part, :]

    h_y = [
        remote(hv.at[part, hcols], hv.at[part, hcols], hys.at[k - 1], hyr.at[k - 1], at(y=yp(k)))
        for k in range(1, NY)
    ]

    @pl.when(head_chip)
    def _():
        for copy in h_y:
            copy.start()

    qv[z, part, span(y * 128, 128)] = encode_chol(blk[part, :])
    mine = qv.at[z, part, span(y * 128, 128)]
    q_y = [remote(mine, mine, qys.at[k - 1], qyr.at[k - 1], at(y=yp(k))) for k in range(1, NY)]
    for copy in q_y:
        copy.start()

    @pl.when(owner_side & not_owner)
    def _():
        for s in range(2):
            scattered(s).wait_recv()
            across(s).start()
        for s in range(2):
            start_share(s)

    @pl.when(owner)
    def _():
        for a in range(2):
            for k in range(1, NX):
                scatter(a, k).wait_send()
        for a in range(2):
            for k in (2, 1, 3):
                share_owner(a, k).start()

    @pl.when(z == 0)
    def _():
        for k in range(1, NY):
            yo = yp(NY - k)
            cols = span(jnp.minimum(yo, 1) * 128, 128)

            @pl.when(yo < 2)
            def _():
                remote(hv.at[part, cols], hv.at[part, cols], hys.at[k - 1], hyr.at[k - 1], at(y=yp(k))).wait_recv()

    h_z = [remote(hv.at[part], hv.at[part], hzs.at[k - 1], hzr.at[0], at(z=zp(k))) for k in range(1, NZ)]

    @pl.when(z == 0)
    def _():
        for k in (4, 3, 5, 2, 6, 1, 7):
            h_z[k - 1].start()

    for k in range(1, NY):
        src = qv.at[z, part, span(yp(NY - k) * 128, 128)]
        remote(src, src, qys.at[k - 1], qyr.at[k - 1], at(y=yp(k))).wait_recv()

    def over_z(k):
        return remote(qv.at[z, part], qv.at[z, part], qzs.at[k - 1], qzr.at[k - 1], at(z=zp(k)))

    def came_over_z(k):
        src = qv.at[zp(NZ - k), part]
        return remote(src, src, qzs.at[k - 1], qzr.at[k - 1], at(z=zp(k)))

    def over_x(j, k):
        src = qv.at[zp(ORDER[j]), part]
        return remote(src, src, qxs.at[j * 3 + k - 1], qxr.at[j * 3 + k - 1], at(x=xp(k)))

    def start_over_x(j):
        if j:
            came_over_z(NZ - ORDER[j]).wait_recv()
        for k in (2, 1, 3):
            over_x(j, k).start()

    for k in (1, 7, 2, 6, 3, 5, 4):
        over_z(k).start()

    load_w.wait()
    load_k.wait()
    wpad[...] = jnp.zeros_like(wpad)
    wpad[0:ROWS, :] = wv[:, 0:PANEL_W].astype(F32)
    kpad[...] = jnp.zeros_like(kpad)
    kpad[0:64, 0:ROWS] = kv[...].astype(F32)
    ct[...] = contract(identity(PANEL_W, BF16), wpad[...].astype(BF16), 1, 1)
    col_id = lax.broadcasted_iota(jnp.int32, (PANEL_W, LANES), 0)
    group_id = lax.broadcasted_iota(jnp.int32, (PANEL_W, LANES), 1)
    repeat = jnp.where(col_id // 4 == group_id, 1.0, 0.0).astype(BF16)
    choice = contract(repeat, kpad[...].astype(BF16), 1, 0).astype(jnp.int32)
    place = col_id % 4
    drop = (
        ((place == 0) & (choice >= 3))
        | ((place == 1) & ((choice == 1) | (choice == 2) | (choice == 5)))
        | ((place == 2) & ((choice == 0) | (choice == 2) | (choice == 4)))
        | ((place == 3) & ((choice == 0) | (choice == 1) | (choice == 3)))
    )
    av[...] = jnp.where(drop, 1.0, 0.0)

    @pl.when(jnp.logical_not(owner_side))
    def _():
        for s in range(2):
            across(s).wait_recv()
            start_share(s)

    @pl.when(z > 0)
    def _():
        h_z[0].wait_recv()

    h_x = [remote(hv.at[part], hv.at[part], hxs.at[k - 1], hxr.at[k - 1], at(x=xp(k))) for k in range(1, NX)]
    for copy in h_x:
        copy.start()

    def gram_part(s):
        @pl.when(not_owner)
        def _():
            for k in range(1, NX):
                shared(s, k).wait_recv()

        for tile in range(4):
            cols = slice(tile * 512, tile * 512 + 512)
            value = contract(pt[s], xv[s, :, cols], 1, 0)
            gv[tile] = value if s == 0 else gv[tile] + value

    @pl.when(owner)
    def _():
        swap_p.wait_recv()

    remote(xv.at[1 - c], xv.at[1 - c], xcs.at[1], xcr.at[1], at(c=1 - c)).wait_recv()
    gram_part(0)
    gram_part(1)

    def own_rows(zd):
        rows = span(zd * 16, 16)
        parts = [gv[tile, rows, :] for tile in range(4)]
        return [p[:, 128 * i : 128 * i + 128] for p in parts for i in range(4)]

    def place_of(tile):
        return tile if tile < 8 else tile + 1

    def pack(tiles, slot):
        most = jnp.abs(tiles[0])
        for value in tiles[1:]:
            most = jnp.maximum(most, jnp.abs(value))
        most = jnp.max(most, axis=0, keepdims=True)
        power = jnp.ceil(jnp.log2(jnp.maximum(most, 1e-30)))
        up = jnp.exp2(-power) * SUM_MAX
        for i, value in enumerate(tiles):
            msend[slot, place_of(i)] = jnp.round(value * up).astype(jnp.int32).astype(jnp.int16)
        msend[slot, 8] = jnp.broadcast_to(power, (16, 128)).astype(jnp.int32).astype(jnp.int16)

    def add(tiles, slot, low=0, high=16):
        down = jnp.exp2(mrecv[slot, 8].astype(jnp.int32).astype(F32)) * (1.0 / SUM_MAX)
        return [
            value + mrecv[slot, place_of(i)].astype(jnp.int32).astype(F32) * down if low <= i < high else value
            for i, value in enumerate(tiles)
        ]

    def message(slot_from, slot_to, k, which=None):
        src, dst = msend.at[slot_from], mrecv.at[slot_to]
        if which is not None:
            src, dst = src.at[pl.ds(8 * which, 9)], dst.at[pl.ds(8 * which, 9)]
        return remote(src, dst, rzs.at[slot_to], rzr.at[slot_to], at(z=zp(k)))

    far = [message(0, 0, 1), message(1, 1, -1), message(2, 2, 2, 0), message(2, 3, -2, 1)]
    near = [message(3, 4, 1), message(4, 5, -1)]
    second = [message(5, 6, 2), message(6, 7, -2)]
    pack(own_rows(zp(4)), 2)
    far[2].start()
    far[3].start()
    pack(own_rows(zp(3)), 0)
    far[0].start()
    pack(own_rows(zp(-3)), 1)
    far[1].start()
    for j in range(3):
        start_over_x(j)
    pack(own_rows(zp(1)), 3)
    near[0].start()
    pack(own_rows(zp(-1)), 4)
    near[1].start()

    for k in range(1, NX):
        rows = span(c * 128 + xp(NX - k) * PART, PART)
        remote(hv.at[rows], hv.at[rows], hxs.at[k - 1], hxr.at[k - 1], at(x=xp(k))).wait_recv()
    h_c = remote(hv.at[half], hv.at[half], hs.at[0], hr.at[0], at(c=1 - c))
    h_c.start()

    for j in range(3, NZ):
        start_over_x(j)

    remote(hv.at[other], hv.at[other], hs.at[0], hr.at[0], at(c=1 - c)).wait_recv()
    head = hv[...]
    row_id = lax.broadcasted_iota(jnp.int32, (PANEL_W, PANEL_W), 0)
    lane_id = lax.broadcasted_iota(jnp.int32, (PANEL_W, PANEL_W), 1)
    pivot = jnp.sum(jnp.where(row_id == lane_id, head, 0.0), axis=1, keepdims=True)
    av[...] = av[...] * (1.0 / pivot)
    upper = jnp.where(lane_id > row_id, head, 0.0).T
    for b in range(PANEL_W // BLOCK):
        at_b = b * BLOCK
        dg[b, :, 0:BLOCK] = upper[at_b : at_b + BLOCK, at_b : at_b + BLOCK]

    def sweep(b, carry):
        rows = span(b * BLOCK, BLOCK)
        factor = av[rows, :]
        corner = dg[b]
        now = ct[rows, :]
        cols = [now[8 * v : 8 * v + 8, :] for v in range(BLOCK // 8)]
        for j in range(BLOCK):
            v0 = j // 8
            err = cols[v0][j % 8 : j % 8 + 1, :] * factor[j : j + 1, :]
            for v in range(v0, BLOCK // 8):
                cols[v] = cols[v] - corner[8 * v : 8 * v + 8, j : j + 1] * err
        done = jnp.concatenate(cols, axis=0)
        errors = done * factor
        et[rows, :] = errors
        update = contract(hv[rows, :], errors, 0, 0, HIGHEST)
        later = col_id >= (b + 1) * BLOCK
        ct[...] = ct[...] - jnp.where(later, update, 0.0)
        ct[rows, :] = done
        return carry

    lax.fori_loop(0, 4, sweep, 0)

    for copy in far:
        copy.wait_recv()
    pack(add(add(own_rows(zp(2)), 0), 2, 0, 8), 5)
    second[0].start()
    pack(add(add(own_rows(zp(-2)), 1), 3, 8, 16), 6)
    second[1].start()

    lax.fori_loop(4, PANEL_W // BLOCK, sweep, 0)
    kept = jnp.where(drop, 0.0, ct[...]).astype(BF16)
    eye = identity(PANEL_W, BF16)
    kept_rows = contract(kept, eye, 0, 0)
    errors = et[...]
    errors_hi = errors.astype(BF16)
    errors_lo = (errors - errors_hi.astype(F32)).astype(BF16)
    eh[...] = contract(errors_hi, eye, 0, 0).astype(BF16)
    el[...] = contract(errors_lo, eye, 0, 0).astype(BF16)

    def block_z(j):
        rel = jnp.where(j % 2 == 1, (j + 1) // 2, (NZ - j // 2) % NZ)
        return lax.rem(z + rel, NZ)

    def between(j, rows):
        src = qv.at[block_z(j), rows]
        return remote(src, src, qcs.at[j], qcr.at[j], at(c=1 - c))

    def hand_over(j):
        for k in range(1, NX):
            src = qv.at[block_z(j), span(c * 128 + xp(NX - k) * PART, PART)]
            remote(src, src, qxs.at[j * 3 + k - 1], qxr.at[j * 3 + k - 1], at(x=xp(k))).wait_recv()
        between(j, half).start()

    for copy in near + second:
        copy.wait_recv()
    tiles = own_rows(z)
    for slot in range(4, 8):
        tiles = add(tiles, slot)
    for tile in range(4):
        summed = jnp.concatenate(tiles[4 * tile : 4 * tile + 4], axis=1)
        for yd in range(NY):
            ysend[yd, tile * 4 : tile * 4 + 4, :] = summed[yd * 4 : yd * 4 + 4, :]
    r_y = [
        remote(ysend.at[yp(k)], yrecv.at[k - 1], rys.at[k - 1], ryr.at[k - 1], at(y=yp(k)))
        for k in range(1, NY)
    ]
    for copy in r_y:
        copy.start()

    hand_over(0)
    hand_over(1)
    hand_over(2)

    def tail(j, carry):
        @pl.when(j + 3 < NZ)
        def _():
            hand_over(j + 3)

        between(j, other).wait_recv()
        zb = block_z(j)
        for i in range(2):
            chol = decode_chol(qv[zb, :, 256 * i : 256 * i + 256])
            chol_hi = chol.astype(BF16)
            chol_lo = (chol - chol_hi.astype(F32)).astype(BF16)
            update = contract(eh[...], chol_hi, 1, 0) + (
                contract(eh[...], chol_lo, 1, 0) + contract(el[...], chol_hi, 1, 0)
            )
            cols = span(zb * 512 + i * 256, 256)
            pruned[:, cols] = (wv[:, cols].astype(F32) - update[0:ROWS, :]).astype(BF16)
        return carry

    lax.fori_loop(0, NZ, tail, 0)
    pruned[:, 0:PANEL_W] = kept_rows[0:ROWS, :].astype(BF16)

    for copy in r_y:
        copy.wait_recv()
    total = ysend[y] + yrecv[0] + yrecv[1] + yrecv[2]
    total = total * (2.0 / (TOK * NZ * NY * NC))
    for tile in range(4):
        gram[:, tile * 512 : tile * 512 + 512] = total[tile * 4 : tile * 4 + 4, :]

    @pl.when(owner)
    def _():
        swap_p.wait_send()
        for a in range(2):
            across_owner(a).wait_send()
            for k in range(1, NX):
                share_owner(a, k).wait_send()

    for s in range(2):
        pl.when(owner_side & not_owner)(across(s).wait_send)
        for k in range(1, NX):
            pl.when(not_owner & jnp.logical_not(to_owner(k)))(share(s, k).wait_send)

    @pl.when(head_chip)
    def _():
        for copy in h_y:
            copy.wait_send()

    @pl.when(z == 0)
    def _():
        for copy in h_z:
            copy.wait_send()

    for copy in [pair, h_c, swap_x] + q_y + h_x + far + near + second + r_y:
        copy.wait_send()
    for k in range(1, NZ):
        over_z(k).wait_send()
    for j in range(NZ):
        for k in range(1, NX):
            over_x(j, k).wait_send()
        between(j, half).wait_send()


def shards(calib_inputs, weights, inverse_chol, keep_pattern):
    dma = pltpu.SemaphoreType.DMA
    vmem = pltpu.VMEM
    scratch = [
        vmem((NC, TOK, FEAT), BF16),
        vmem((TOK, PANEL_W), BF16),
        vmem((ROWS, WINDOW), BF16),
        vmem((64, ROWS), jnp.int32),
        vmem((64, PANEL_W), F32),
        vmem((64, PANEL_W), F32),
        vmem((PANEL_W, 128), F32),
        vmem((NZ, PANEL_W, NY * 128), jnp.int16),
        vmem((PANEL_W, PANEL_W), F32),
        vmem((4, 128, 512), F32),
        vmem((7, 17, 16, 128), jnp.int16),
        vmem((8, 17, 16, 128), jnp.int16),
        vmem((NY, 16, 512), F32),
        vmem((NY - 1, 16, 512), F32),
        vmem((LANES, PANEL_W), F32),
        vmem((LANES, LANES), F32),
        vmem((PANEL_W // BLOCK, BLOCK, 128), F32),
        vmem((PANEL_W, LANES), F32),
        vmem((PANEL_W, LANES), F32),
        vmem((PANEL_W, LANES), F32),
        vmem((LANES, PANEL_W), BF16),
        vmem((LANES, PANEL_W), BF16),
        vmem((PANEL_W, TOK), BF16),
        vmem((NC, 128, TOK), BF16),
    ]
    sems = [5, 2, 6, 2, 2, 2, 6, 6, 3, 3, 7, 7, 24, 24, 8, 8, 3, 3, 7, 1, 3, 3, 1, 1, 2, 2, 8, 8, 3, 3]
    scratch += [dma((n,)) for n in sems]
    anywhere = pl.BlockSpec(memory_space=pltpu.HBM)
    inside = pl.BlockSpec(memory_space=pltpu.VMEM)
    return pl.pallas_call(
        kernel,
        out_shape=(
            pltpu.VMEM((ROWS, WINDOW), BF16),
            pltpu.VMEM((PANEL_W // (NZ * NY * NC), FEAT), F32),
        ),
        in_specs=[anywhere] * 4,
        out_specs=(inside, inside),
        scratch_shapes=scratch,
        compiler_params=pltpu.CompilerParams(
            collective_id=0, has_side_effects=True, vmem_limit_bytes=40 * 2**20
        ),
        cost_estimate=pl.CostEstimate(flops=2 * 10**9, bytes_accessed=8 * 10**6, transcendentals=0),
    )(*[pltpu.with_memory_space_constraint(v, pltpu.HBM) for v in (calib_inputs, weights, inverse_chol.T, keep_pattern.T)])


def solution(mesh):
    placed = (
        P("dp", "tensor"),
        P(("dp", "tensor"), None),
        P(None, "dp"),
        P(("dp", "tensor"), None),
    )
    return jax.shard_map(
        shards,
        mesh=mesh,
        in_specs=placed,
        out_specs=(P(("dp", "tensor"), None), P("dp", "tensor")),
        check_vma=False,
    )
```

```python
import jax
import jax.numpy as jnp
from jax import lax
from jax.experimental import pallas as pl
from jax.experimental.pallas import tpu as pltpu
from jax.sharding import PartitionSpec as P

MESH = pl.DeviceIdType.MESH
NZ, NY, NC, NH, NX = 8, 4, 2, 2, 4
PANEL_W = 256
WINDOW = 4096
ROWS = 104
LANES = 128
FEAT = 2048
TOK = 768
QTOK = TOK // NX
PART = PANEL_W // (NX * NC)
SHARE = PANEL_W // (2 * NC)
OWNER_X, OWNER_H = 2, 1
BLOCK = 32
CODE_MAX = 32767.0
CHOL_MAX = 2.0
SUM_MAX = 32000.0
F32 = jnp.float32
BF16 = jnp.bfloat16
HIGHEST = lax.Precision.HIGHEST


def contract(a, b, da, db, precision=None):
    return lax.dot_general(
        a, b, (((da,), (db,)), ((), ())), precision=precision, preferred_element_type=F32
    )


def identity(n, dtype):
    rows = lax.broadcasted_iota(jnp.int32, (n, n), 0)
    cols = lax.broadcasted_iota(jnp.int32, (n, n), 1)
    return jnp.where(rows == cols, 1.0, 0.0).astype(dtype)


def panel_order():
    rows = lax.broadcasted_iota(jnp.int32, (PANEL_W, PANEL_W), 0)
    cols = lax.broadcasted_iota(jnp.int32, (PANEL_W, PANEL_W), 1)
    core, rest = rows // 128, rows % 128
    feature = (rest // 4) * 8 + core * 4 + rest % 4
    return jnp.where(feature == cols, 1.0, 0.0).astype(BF16)


def encode_chol(value):
    root = jnp.sqrt(jnp.minimum(jnp.abs(value) * (1.0 / CHOL_MAX), 1.0)) * CODE_MAX
    code = jnp.round(jnp.where(value < 0.0, -root, root))
    return code.astype(jnp.int32).astype(jnp.int16)


def decode_chol(code):
    value = code.astype(jnp.int32).astype(F32)
    return value * jnp.abs(value) * (CHOL_MAX / (CODE_MAX * CODE_MAX))


ORDER = (0, 1, 7, 2, 6, 3, 5, 4)
GROUPS = ((0, 1), (1, 2), (2, 3), (3, 4), (4, 5), (5, 6), (6, 7), (7, 8))


def kernel(
    calib, weights, inverse, pattern,
    pruned, gram,
    xv, pv, wv, kv, iv, ipeer, blk, qv, hv, gv, msend, mrecv, ysend, yrecv,
    wpad, kpad, dg, ct, av, et, eh, el, po, pt,
    lsem, isem, s1s, s1r, hcs, hcr, s2s, s2r,
    qys, qyr, qzs, qzr, qxs, qxr, qcs, qcr, hys, hyr, hzs, hzr, hxs, hxr, hs, hr,
    xcs, xcr, rzs, rzr, rys, ryr,
):
    d = lax.axis_index("dp")
    t = lax.axis_index("tensor")
    z, y, c = d // (NY * NC), (d // NC) % NY, d % NC
    h, x = t // NX, t % NX
    owner = (h == OWNER_H) & (x == OWNER_X)
    not_owner = jnp.logical_not(owner)
    owner_side = h == OWNER_H

    def at(z=z, y=y, c=c, h=h, x=x):
        return ((z * NY + y) * NC + c, h * NX + x)

    def remote(src, dst, send, recv, where):
        return pltpu.make_async_remote_copy(
            src_ref=src, dst_ref=dst, send_sem=send, recv_sem=recv,
            device_id=where, device_id_type=MESH,
        )

    def zp(k):
        return lax.rem(z + k + NZ, NZ)

    def yp(k):
        return lax.rem(y + k, NY)

    def xp(k):
        return lax.rem(x + k, NX)

    def span(start, size):
        return pl.ds(pl.multiple_of(start, size), size)

    load_i = pltpu.make_async_copy(inverse, iv, lsem.at[0])
    load_x = pltpu.make_async_copy(calib, xv.at[c], lsem.at[1])
    load_w = pltpu.make_async_copy(weights, wv, lsem.at[2])
    load_k = pltpu.make_async_copy(pattern, kv, lsem.at[3])
    load_p = pltpu.make_async_copy(calib.at[:, pl.ds(0, PANEL_W)], pv, lsem.at[4])
    pl.when(owner)(load_p.start)
    load_i.start()
    load_x.start()
    load_w.start()
    load_k.start()

    barrier = pltpu.get_barrier_semaphore()
    partners = [at(x=xp(k), c=c) for k in range(1, NX)] + [at(x=xp(k), c=1 - c) for k in range(1, NX)]
    partners += [at(h=1 - h), at(h=1 - h, c=1 - c), at(c=1 - c)]
    partners += [at(y=yp(k)) for k in range(1, NY)]
    partners += [at(z=zp(k)) for k in range(1, NZ)]
    for partner in partners:
        pl.semaphore_signal(barrier, inc=1, device_id=partner, device_id_type=MESH)

    @pl.when(owner)
    def _():
        load_p.wait()
        po[...] = contract(panel_order(), pv[...], 1, 1).astype(BF16)
        pt[c] = po[span(c * 128, 128), :]

    load_i.wait()
    pl.semaphore_wait(barrier, len(partners))

    def ordered(a, xo):
        return po.at[span(a * 128 + xo * PART, PART)]

    def piece(s, xo):
        return pt.at[s, span(xo * PART, PART)]

    def scatter(a, k):
        return remote(ordered(a, xp(k)), piece(c, xp(k)), s1s.at[a * 3 + k - 1], s1r.at[c], at(x=xp(k), c=a))

    def scattered(s):
        return remote(piece(s, x), piece(s, x), s1s.at[s], s1r.at[s], at(x=xp(1)))

    def across_owner(a, u):
        src = po.at[span(a * 128 + x * PART + u * 16, 16)]
        return remote(src, sub(c, x, u), hcs.at[a * 2 + u], hcr.at[c * 2 + u], at(h=1 - h, c=a))

    def sub(s, xo, u):
        return pt.at[s, span(xo * PART + u * 16, 16)]

    def across(s, u):
        sem = s * 2 + u
        return remote(sub(s, x, u), sub(s, x, u), hcs.at[sem], hcr.at[sem], at(h=1 - h))

    def share_owner(a, k, u):
        src = po.at[span(a * 128 + x * PART + u * 16, 16)]
        sem = s2r.at[(c * 3 + k - 1) * 2 + u]
        return remote(src, sub(c, x, u), s2s.at[(a * 3 + k - 1) * 2 + u], sem, at(x=xp(k), c=a))

    def share(s, k, u):
        sem = (s * 3 + k - 1) * 2 + u
        return remote(sub(s, x, u), sub(s, x, u), s2s.at[sem], s2r.at[sem], at(x=xp(k)))

    def shared(s, k, u):
        src = sub(s, xp(NX - k), u)
        sem = (s * 3 + k - 1) * 2 + u
        return remote(src, src, s2s.at[sem], s2r.at[sem], at(x=xp(k)))

    swap_p = remote(po.at[span((1 - c) * 128, 128)], pt.at[c], xcs.at[0], xcr.at[0], at(c=1 - c))
    swap_x = remote(xv.at[c], xv.at[c], xcs.at[1], xcr.at[1], at(c=1 - c))

    def to_owner(k):
        return owner_side & (xp(k) == OWNER_X)

    def start_share(s, u):
        for k in (2, 1, 3):
            pl.when(jnp.logical_not(to_owner(k)))(share(s, k, u).start)

    pair = remote(iv, ipeer, isem.at[0], isem.at[1], at(c=1 - c))
    pair.start()

    @pl.when(owner)
    def _():
        for a in range(2):
            for k in (2, 1, 3):
                scatter(a, k).start()
            for u in range(2):
                across_owner(a, u).start()
        swap_p.start()

    load_x.wait()
    swap_x.start()

    part = span(c * 128 + (x % 2) * SHARE, SHARE)

    def lower(parity):
        return span(c * 128 + parity * SHARE, SHARE // 2)

    def upper_of(parity):
        return span(c * 128 + parity * SHARE + SHARE // 2, SHARE // 2)

    even_x = x % 2
    lends = (lower(even_x), upper_of(even_x))
    lacks = (lower(1 - even_x), upper_of(1 - even_x))
    sides = (xp(1), xp(3))
    half = span(c * 128, 128)
    other = span((1 - c) * 128, 128)
    head_chip = (z == 0) & (y < 2)
    hcols = span(jnp.minimum(y, 1) * 128, 128)

    pair.wait_recv()
    even = jnp.full(iv.shape, c, jnp.int32) == 0
    blk[...] = jnp.concatenate(
        [jnp.where(even, iv[...], ipeer[...]), jnp.where(even, ipeer[...], iv[...])], axis=0
    ).T

    @pl.when(head_chip)
    def _():
        hv[part, hcols] = blk[part, :]

    h_y = [
        remote(hv.at[part, hcols], hv.at[part, hcols], hys.at[k - 1], hyr.at[k - 1], at(y=yp(k)))
        for k in range(1, NY)
    ]

    @pl.when(head_chip)
    def _():
        for copy in h_y:
            copy.start()

    qv[0, part, span(y * 128, 128)] = encode_chol(blk[part, :])
    mine = qv.at[0, part, span(y * 128, 128)]
    q_y = [remote(mine, mine, qys.at[k - 1], qyr.at[k - 1], at(y=yp(k))) for k in range(1, NY)]
    for copy in q_y:
        copy.start()

    @pl.when(owner_side & not_owner)
    def _():
        for s in range(2):
            scattered(s).wait_recv()
            for u in range(2):
                across(s, u).start()
        for s in range(2):
            for u in range(2):
                start_share(s, u)

    @pl.when(owner)
    def _():
        for a in range(2):
            for k in range(1, NX):
                scatter(a, k).wait_send()
        for a in range(2):
            for k in (2, 1, 3):
                for u in range(2):
                    share_owner(a, k, u).start()

    @pl.when(z == 0)
    def _():
        for k in range(1, NY):
            yo = yp(NY - k)
            cols = span(jnp.minimum(yo, 1) * 128, 128)

            @pl.when(yo < 2)
            def _():
                remote(hv.at[part, cols], hv.at[part, cols], hys.at[k - 1], hyr.at[k - 1], at(y=yp(k))).wait_recv()

    h_z = [remote(hv.at[part], hv.at[part], hzs.at[k - 1], hzr.at[0], at(z=zp(k))) for k in range(1, NZ)]

    @pl.when(z == 0)
    def _():
        for k in (4, 3, 5, 2, 6, 1, 7):
            h_z[k - 1].start()

    for k in range(1, NY):
        src = qv.at[0, part, span(yp(NY - k) * 128, 128)]
        remote(src, src, qys.at[k - 1], qyr.at[k - 1], at(y=yp(k))).wait_recv()

    def block(rel, rows=part):
        return qv.at[ORDER.index(rel % NZ), rows]

    def over_z(n, k):
        return remote(block(0), block(-k), qzs.at[n], qzr.at[n], at(z=zp(k)))

    def came_over_z(n, k):
        return remote(block(-k), block(-k), qzs.at[n], qzr.at[n], at(z=zp(k)))

    def onward(n, k):
        return remote(block(-2 * k), block(-3 * k), qzs.at[4 + n], qzr.at[4 + n], at(z=zp(k)))

    def onward_half(n, k):
        rows = span(c * 128 + even_x * SHARE + n * (SHARE // 2), SHARE // 2)
        return remote(block(-2 * k, rows), block(4, rows), qzs.at[6 + n], qzr.at[6 + n], at(z=zp(2 * k)))

    first_z = ((0, 2), (1, -2), (2, 1), (3, -1))

    def came_onward(rel):
        if rel == 4:
            for n in range(2):
                rows = span(c * 128 + even_x * SHARE + n * (SHARE // 2), SHARE // 2)
                remote(block(4, rows), block(4, rows), qzs.at[6 + n], qzr.at[6 + n], at(z=zp(1))).wait_recv()
        elif rel in (3, 5):
            n = 1 if rel == 3 else 0
            remote(block(rel), block(rel), qzs.at[4 + n], qzr.at[4 + n], at(z=zp(1))).wait_recv()
        elif rel in (1, 7):
            n = 2 if rel == 7 else 3
            came_over_z(n, first_z[n][1]).wait_recv()

    def group(g, rows):
        low, high = GROUPS[g]
        return qv.at[pl.ds(low, high - low), rows]

    def over_x(g, n):
        src = group(g, lends[n])
        return remote(src, src, qxs.at[g * 2 + n], qxr.at[g * 2 + n], at(x=sides[n]))

    def start_over_x(g):
        for j in range(*GROUPS[g]):
            came_onward(ORDER[j])
        for n in range(2):
            over_x(g, n).start()

    for n, k in first_z:
        over_z(n, k).start()

    load_w.wait()
    load_k.wait()
    wpad[...] = jnp.zeros_like(wpad)
    wpad[0:ROWS, :] = wv[:, 0:PANEL_W].astype(F32)
    kpad[...] = jnp.zeros_like(kpad)
    kpad[0:64, 0:ROWS] = kv[...].astype(F32)
    ct[...] = contract(identity(PANEL_W, BF16), wpad[...].astype(BF16), 1, 1)
    col_id = lax.broadcasted_iota(jnp.int32, (PANEL_W, LANES), 0)
    group_id = lax.broadcasted_iota(jnp.int32, (PANEL_W, LANES), 1)
    repeat = jnp.where(col_id // 4 == group_id, 1.0, 0.0).astype(BF16)
    choice = contract(repeat, kpad[...].astype(BF16), 1, 0).astype(jnp.int32)
    place = col_id % 4
    drop = (
        ((place == 0) & (choice >= 3))
        | ((place == 1) & ((choice == 1) | (choice == 2) | (choice == 5)))
        | ((place == 2) & ((choice == 0) | (choice == 2) | (choice == 4)))
        | ((place == 3) & ((choice == 0) | (choice == 1) | (choice == 3)))
    )
    av[...] = jnp.where(drop, 1.0, 0.0)

    @pl.when(jnp.logical_not(owner_side))
    def _():
        for s in range(2):
            for u in range(2):
                across(s, u).wait_recv()
                start_share(s, u)

    for n, k in ((0, 1), (1, -1)):
        came_over_z(n, 2 * k).wait_recv()
        onward(n, k).start()
        onward_half(n, k).start()

    @pl.when(z > 0)
    def _():
        h_z[0].wait_recv()

    h_x = [remote(hv.at[lends[n]], hv.at[lends[n]], hxs.at[n], hxr.at[n], at(x=sides[n])) for n in range(2)]
    for copy in h_x:
        copy.start()

    def gram_part(s):
        @pl.when(not_owner)
        def _():
            for k in range(1, NX):
                for u in range(2):
                    shared(s, k, u).wait_recv()

        for tile in range(4):
            cols = slice(tile * 512, tile * 512 + 512)
            value = contract(pt[s], xv[s, :, cols], 1, 0)
            gv[tile] = value if s == 0 else gv[tile] + value

    @pl.when(owner)
    def _():
        swap_p.wait_recv()

    remote(xv.at[1 - c], xv.at[1 - c], xcs.at[1], xcr.at[1], at(c=1 - c)).wait_recv()
    gram_part(0)
    gram_part(1)

    def own_rows(zd):
        rows = span(zd * 16, 16)
        parts = [gv[tile, rows, :] for tile in range(4)]
        return [p[:, 128 * i : 128 * i + 128] for p in parts for i in range(4)]

    def place_of(tile):
        return tile if tile < 8 else tile + 1

    def pack(tiles, slot):
        most = jnp.abs(tiles[0])
        for value in tiles[1:]:
            most = jnp.maximum(most, jnp.abs(value))
        most = jnp.max(most, axis=0, keepdims=True)
        power = jnp.ceil(jnp.log2(jnp.maximum(most, 1e-30)))
        up = jnp.exp2(-power) * SUM_MAX
        for i, value in enumerate(tiles):
            msend[slot, place_of(i)] = jnp.round(value * up).astype(jnp.int32).astype(jnp.int16)
        msend[slot, 8] = jnp.broadcast_to(power, (16, 128)).astype(jnp.int32).astype(jnp.int16)

    def add(tiles, slot, low=0, high=16):
        down = jnp.exp2(mrecv[slot, 8].astype(jnp.int32).astype(F32)) * (1.0 / SUM_MAX)
        return [
            value + mrecv[slot, place_of(i)].astype(jnp.int32).astype(F32) * down if low <= i < high else value
            for i, value in enumerate(tiles)
        ]

    def message(slot_from, slot_to, k, which=None):
        src, dst = msend.at[slot_from], mrecv.at[slot_to]
        if which is not None:
            src, dst = src.at[pl.ds(8 * which, 9)], dst.at[pl.ds(8 * which, 9)]
        return remote(src, dst, rzs.at[slot_to], rzr.at[slot_to], at(z=zp(k)))

    far = [message(0, 0, 1), message(1, 1, -1), message(2, 2, 2, 0), message(2, 3, -2, 1)]
    near = [message(3, 4, 1), message(4, 5, -1)]
    second = [message(5, 6, 2), message(6, 7, -2)]
    pack(own_rows(zp(4)), 2)
    far[2].start()
    far[3].start()
    pack(own_rows(zp(3)), 0)
    far[0].start()
    pack(own_rows(zp(-3)), 1)
    far[1].start()
    pack(own_rows(zp(1)), 3)
    near[0].start()
    pack(own_rows(zp(-1)), 4)
    near[1].start()

    start_over_x(0)
    for n in range(2):
        remote(hv.at[lacks[n]], hv.at[lacks[n]], hxs.at[n], hxr.at[n], at(x=sides[n])).wait_recv()
    h_c = remote(hv.at[half], hv.at[half], hs.at[0], hr.at[0], at(c=1 - c))
    h_c.start()

    for g in range(1, len(GROUPS)):
        start_over_x(g)

    remote(hv.at[other], hv.at[other], hs.at[0], hr.at[0], at(c=1 - c)).wait_recv()
    head = hv[...]
    row_id = lax.broadcasted_iota(jnp.int32, (PANEL_W, PANEL_W), 0)
    lane_id = lax.broadcasted_iota(jnp.int32, (PANEL_W, PANEL_W), 1)
    pivot = jnp.sum(jnp.where(row_id == lane_id, head, 0.0), axis=1, keepdims=True)
    av[...] = av[...] * (1.0 / pivot)
    upper = jnp.where(lane_id > row_id, head, 0.0).T
    for b in range(PANEL_W // BLOCK):
        at_b = b * BLOCK
        dg[b, :, 0:BLOCK] = upper[at_b : at_b + BLOCK, at_b : at_b + BLOCK]

    def sweep(b, carry):
        rows = span(b * BLOCK, BLOCK)
        factor = av[rows, :]
        corner = dg[b]
        now = ct[rows, :]
        cols = [now[8 * v : 8 * v + 8, :] for v in range(BLOCK // 8)]
        for j in range(BLOCK):
            v0 = j // 8
            err = cols[v0][j % 8 : j % 8 + 1, :] * factor[j : j + 1, :]
            for v in range(v0, BLOCK // 8):
                cols[v] = cols[v] - corner[8 * v : 8 * v + 8, j : j + 1] * err
        done = jnp.concatenate(cols, axis=0)
        errors = done * factor
        et[rows, :] = errors
        update = contract(hv[rows, :], errors, 0, 0, HIGHEST)
        later = col_id >= (b + 1) * BLOCK
        ct[...] = ct[...] - jnp.where(later, update, 0.0)
        ct[rows, :] = done
        return carry

    lax.fori_loop(0, 2, sweep, 0)
    lax.fori_loop(2, 4, sweep, 0)

    for copy in far:
        copy.wait_recv()
    pack(add(add(own_rows(zp(2)), 0), 2, 0, 8), 5)
    second[0].start()
    pack(add(add(own_rows(zp(-2)), 1), 3, 8, 16), 6)
    second[1].start()

    lax.fori_loop(4, PANEL_W // BLOCK, sweep, 0)
    kept = jnp.where(drop, 0.0, ct[...]).astype(BF16)
    eye = identity(PANEL_W, BF16)
    kept_rows = contract(kept, eye, 0, 0)
    errors = et[...]
    errors_hi = errors.astype(BF16)
    errors_lo = (errors - errors_hi.astype(F32)).astype(BF16)
    eh[...] = contract(errors_hi, eye, 0, 0).astype(BF16)
    el[...] = contract(errors_lo, eye, 0, 0).astype(BF16)

    def block_z(j):
        rel = jnp.where(j % 2 == 1, (j + 1) // 2, (NZ - j // 2) % NZ)
        return lax.rem(z + rel, NZ)

    def between(g, rows):
        src = group(g, rows)
        return remote(src, src, qcs.at[g], qcr.at[g], at(c=1 - c))

    def hand_over(g):
        for n in range(2):
            src = group(g, lacks[n])
            remote(src, src, qxs.at[g * 2 + n], qxr.at[g * 2 + n], at(x=sides[n])).wait_recv()
        between(g, half).start()

    for g in range(8):
        hand_over(g)

    for copy in near + second:
        copy.wait_recv()
    tiles = own_rows(z)
    for slot in range(4, 8):
        tiles = add(tiles, slot)
    for tile in range(4):
        summed = jnp.concatenate(tiles[4 * tile : 4 * tile + 4], axis=1)
        for yd in range(NY):
            ysend[yd, tile * 4 : tile * 4 + 4, :] = summed[yd * 4 : yd * 4 + 4, :]
    r_y = [
        remote(ysend.at[yp(k)], yrecv.at[k - 1], rys.at[k - 1], ryr.at[k - 1], at(y=yp(k)))
        for k in range(1, NY)
    ]
    for copy in r_y:
        copy.start()

    def tail(j, carry):
        zb = block_z(j)
        for i in range(2):
            chol = decode_chol(qv[j, :, 256 * i : 256 * i + 256])
            chol_hi = chol.astype(BF16)
            chol_lo = (chol - chol_hi.astype(F32)).astype(BF16)
            update = contract(eh[...], chol_hi, 1, 0) + (
                contract(eh[...], chol_lo, 1, 0) + contract(el[...], chol_hi, 1, 0)
            )
            cols = span(zb * 512 + i * 256, 256)
            pruned[:, cols] = (wv[:, cols].astype(F32) - update[0:ROWS, :]).astype(BF16)
        return carry

    for g, (low, high) in enumerate(GROUPS):
        if g + 8 < len(GROUPS):
            hand_over(g + 8)
        between(g, other).wait_recv()
        lax.fori_loop(low, high, tail, 0)
    pruned[:, 0:PANEL_W] = kept_rows[0:ROWS, :].astype(BF16)

    for copy in r_y:
        copy.wait_recv()
    total = ysend[y] + yrecv[0] + yrecv[1] + yrecv[2]
    total = total * (2.0 / (TOK * NZ * NY * NC))
    for tile in range(4):
        gram[:, tile * 512 : tile * 512 + 512] = total[tile * 4 : tile * 4 + 4, :]

    @pl.when(owner)
    def _():
        swap_p.wait_send()
        for a in range(2):
            for u in range(2):
                across_owner(a, u).wait_send()
                for k in range(1, NX):
                    share_owner(a, k, u).wait_send()

    for s in range(2):
        for u in range(2):
            pl.when(owner_side & not_owner)(across(s, u).wait_send)
            for k in range(1, NX):
                pl.when(not_owner & jnp.logical_not(to_owner(k)))(share(s, k, u).wait_send)

    @pl.when(head_chip)
    def _():
        for copy in h_y:
            copy.wait_send()

    @pl.when(z == 0)
    def _():
        for copy in h_z:
            copy.wait_send()

    for copy in [pair, h_c, swap_x] + q_y + h_x + far + near + second + r_y:
        copy.wait_send()
    for n, k in first_z:
        over_z(n, k).wait_send()
    for n, k in ((0, 1), (1, -1)):
        onward(n, k).wait_send()
        onward_half(n, k).wait_send()
    for g in range(len(GROUPS)):
        for n in range(2):
            over_x(g, n).wait_send()
        between(g, half).wait_send()


def shards(calib_inputs, weights, inverse_chol, keep_pattern):
    dma = pltpu.SemaphoreType.DMA
    vmem = pltpu.VMEM
    scratch = [
        vmem((NC, TOK, FEAT), BF16),
        vmem((TOK, PANEL_W), BF16),
        vmem((ROWS, WINDOW), BF16),
        vmem((64, ROWS), jnp.int32),
        vmem((64, PANEL_W), F32),
        vmem((64, PANEL_W), F32),
        vmem((PANEL_W, 128), F32),
        vmem((NZ, PANEL_W, NY * 128), jnp.int16),
        vmem((PANEL_W, PANEL_W), F32),
        vmem((4, 128, 512), F32),
        vmem((7, 17, 16, 128), jnp.int16),
        vmem((8, 17, 16, 128), jnp.int16),
        vmem((NY, 16, 512), F32),
        vmem((NY - 1, 16, 512), F32),
        vmem((LANES, PANEL_W), F32),
        vmem((LANES, LANES), F32),
        vmem((PANEL_W // BLOCK, BLOCK, 128), F32),
        vmem((PANEL_W, LANES), F32),
        vmem((PANEL_W, LANES), F32),
        vmem((PANEL_W, LANES), F32),
        vmem((LANES, PANEL_W), BF16),
        vmem((LANES, PANEL_W), BF16),
        vmem((PANEL_W, TOK), BF16),
        vmem((NC, 128, TOK), BF16),
    ]
    sems = [5, 2, 6, 2, 4, 4, 12, 12, 3, 3, 8, 8, 16, 16, 8, 8, 3, 3, 7, 1, 3, 3, 1, 1, 2, 2, 8, 8, 3, 3]
    scratch += [dma((n,)) for n in sems]
    anywhere = pl.BlockSpec(memory_space=pltpu.HBM)
    inside = pl.BlockSpec(memory_space=pltpu.VMEM)
    return pl.pallas_call(
        kernel,
        out_shape=(
            pltpu.VMEM((ROWS, WINDOW), BF16),
            pltpu.VMEM((PANEL_W // (NZ * NY * NC), FEAT), F32),
        ),
        in_specs=[anywhere] * 4,
        out_specs=(inside, inside),
        scratch_shapes=scratch,
        compiler_params=pltpu.CompilerParams(
            collective_id=0, has_side_effects=True, vmem_limit_bytes=40 * 2**20
        ),
        cost_estimate=pl.CostEstimate(flops=2 * 10**9, bytes_accessed=8 * 10**6, transcendentals=0),
    )(*[pltpu.with_memory_space_constraint(v, pltpu.HBM) for v in (calib_inputs, weights, inverse_chol.T, keep_pattern.T)])


def solution(mesh):
    placed = (
        P("dp", "tensor"),
        P(("dp", "tensor"), None),
        P(None, "dp"),
        P(("dp", "tensor"), None),
    )
    return jax.shard_map(
        shards,
        mesh=mesh,
        in_specs=placed,
        out_specs=(P(("dp", "tensor"), None), P("dp", "tensor")),
        check_vma=False,
    )
```

```python
import jax
import jax.numpy as jnp
from jax import lax
from jax.experimental import pallas as pl
from jax.experimental.pallas import tpu as pltpu
from jax.sharding import PartitionSpec as P

MESH = pl.DeviceIdType.MESH
NZ, NY, NC, NH, NX = 8, 4, 2, 2, 4
PANEL_W = 256
WINDOW = 4096
ROWS = 104
LANES = 128
FEAT = 2048
TOK = 768
QTOK = TOK // NX
PART = PANEL_W // (NX * NC)
SHARE = PANEL_W // (2 * NC)
OWNER_X, OWNER_H = 2, 1
BLOCK = 32
CODE_MAX = 32767.0
CHOL_MAX = 2.0
SUM_MAX = 32000.0
F32 = jnp.float32
BF16 = jnp.bfloat16
HIGHEST = lax.Precision.HIGHEST


def contract(a, b, da, db, precision=None):
    return lax.dot_general(
        a, b, (((da,), (db,)), ((), ())), precision=precision, preferred_element_type=F32
    )


def identity(n, dtype):
    rows = lax.broadcasted_iota(jnp.int32, (n, n), 0)
    cols = lax.broadcasted_iota(jnp.int32, (n, n), 1)
    return jnp.where(rows == cols, 1.0, 0.0).astype(dtype)


def panel_order():
    rows = lax.broadcasted_iota(jnp.int32, (PANEL_W, PANEL_W), 0)
    cols = lax.broadcasted_iota(jnp.int32, (PANEL_W, PANEL_W), 1)
    core, rest = rows // 128, rows % 128
    feature = (rest // 4) * 8 + core * 4 + rest % 4
    return jnp.where(feature == cols, 1.0, 0.0).astype(BF16)


def encode_chol(value):
    root = jnp.sqrt(jnp.minimum(jnp.abs(value) * (1.0 / CHOL_MAX), 1.0)) * CODE_MAX
    code = jnp.round(jnp.where(value < 0.0, -root, root))
    return code.astype(jnp.int32).astype(jnp.int16)


def decode_chol(code):
    value = code.astype(jnp.int32).astype(F32)
    return value * jnp.abs(value) * (CHOL_MAX / (CODE_MAX * CODE_MAX))


ORDER = (0, 1, 7, 2, 6, 3, 5, 4)
GROUPS = ((0, 1), (1, 2), (2, 3), (3, 4), (4, 5), (5, 6), (6, 7), (7, 8))


def kernel(
    calib, weights, inverse, pattern,
    pruned, gram,
    xv, pv, wv, kv, iv, ipeer, blk, qv, hv, gv, msend, mrecv, ysend, yrecv,
    wpad, kpad, dg, ct, av, et, eh, el, po, pt,
    lsem, isem, s1s, s1r, hcs, hcr, s2s, s2r,
    qys, qyr, qzs, qzr, qxs, qxr, qcs, qcr, hys, hyr, hzs, hzr, hxs, hxr, hs, hr,
    xcs, xcr, rzs, rzr, rys, ryr,
):
    d = lax.axis_index("dp")
    t = lax.axis_index("tensor")
    z, y, c = d // (NY * NC), (d // NC) % NY, d % NC
    h, x = t // NX, t % NX
    owner = (h == OWNER_H) & (x == OWNER_X)
    not_owner = jnp.logical_not(owner)
    owner_side = h == OWNER_H

    def at(z=z, y=y, c=c, h=h, x=x):
        return ((z * NY + y) * NC + c, h * NX + x)

    def remote(src, dst, send, recv, where):
        return pltpu.make_async_remote_copy(
            src_ref=src, dst_ref=dst, send_sem=send, recv_sem=recv,
            device_id=where, device_id_type=MESH,
        )

    def zp(k):
        return lax.rem(z + k + NZ, NZ)

    def yp(k):
        return lax.rem(y + k, NY)

    def xp(k):
        return lax.rem(x + k, NX)

    def span(start, size):
        return pl.ds(pl.multiple_of(start, size), size)

    load_i = pltpu.make_async_copy(inverse, iv, lsem.at[0])
    load_x = pltpu.make_async_copy(calib, xv.at[c], lsem.at[1])
    load_w = pltpu.make_async_copy(weights, wv, lsem.at[2])
    load_k = pltpu.make_async_copy(pattern, kv, lsem.at[3])
    load_p = pltpu.make_async_copy(calib.at[:, pl.ds(0, PANEL_W)], pv, lsem.at[4])
    pl.when(owner)(load_p.start)
    load_i.start()
    load_x.start()
    load_w.start()
    load_k.start()

    barrier = pltpu.get_barrier_semaphore()
    partners = [at(x=xp(k), c=c) for k in range(1, NX)] + [at(x=xp(k), c=1 - c) for k in range(1, NX)]
    partners += [at(h=1 - h), at(h=1 - h, c=1 - c), at(c=1 - c)]
    partners += [at(y=yp(k)) for k in range(1, NY)]
    partners += [at(z=zp(k)) for k in range(1, NZ)]
    for partner in partners:
        pl.semaphore_signal(barrier, inc=1, device_id=partner, device_id_type=MESH)

    @pl.when(owner)
    def _():
        load_p.wait()
        po[...] = contract(panel_order(), pv[...], 1, 1).astype(BF16)
        pt[c] = po[span(c * 128, 128), :]

    load_i.wait()
    pl.semaphore_wait(barrier, len(partners))

    def ordered(a, xo):
        return po.at[span(a * 128 + xo * PART, PART)]

    def piece(s, xo):
        return pt.at[s, span(xo * PART, PART)]

    def scatter(a, k):
        return remote(ordered(a, xp(k)), piece(c, xp(k)), s1s.at[a * 3 + k - 1], s1r.at[c], at(x=xp(k), c=a))

    def scattered(s):
        return remote(piece(s, x), piece(s, x), s1s.at[s], s1r.at[s], at(x=xp(1)))

    def across_owner(a, u):
        src = po.at[span(a * 128 + x * PART + u * 16, 16)]
        return remote(src, sub(c, x, u), hcs.at[a * 2 + u], hcr.at[c * 2 + u], at(h=1 - h, c=a))

    def sub(s, xo, u):
        return pt.at[s, span(xo * PART + u * 16, 16)]

    def across(s, u):
        sem = s * 2 + u
        return remote(sub(s, x, u), sub(s, x, u), hcs.at[sem], hcr.at[sem], at(h=1 - h))

    def share_owner(a, k, u):
        src = po.at[span(a * 128 + x * PART + u * 16, 16)]
        sem = s2r.at[(c * 3 + k - 1) * 2 + u]
        return remote(src, sub(c, x, u), s2s.at[(a * 3 + k - 1) * 2 + u], sem, at(x=xp(k), c=a))

    def share(s, k, u):
        sem = (s * 3 + k - 1) * 2 + u
        return remote(sub(s, x, u), sub(s, x, u), s2s.at[sem], s2r.at[sem], at(x=xp(k)))

    def shared(s, k, u):
        src = sub(s, xp(NX - k), u)
        sem = (s * 3 + k - 1) * 2 + u
        return remote(src, src, s2s.at[sem], s2r.at[sem], at(x=xp(k)))

    swap_p = remote(po.at[span((1 - c) * 128, 128)], pt.at[c], xcs.at[0], xcr.at[0], at(c=1 - c))
    swap_x = remote(xv.at[c], xv.at[c], xcs.at[1], xcr.at[1], at(c=1 - c))

    def to_owner(k):
        return owner_side & (xp(k) == OWNER_X)

    def start_share(s, u):
        for k in (2, 1, 3):
            pl.when(jnp.logical_not(to_owner(k)))(share(s, k, u).start)

    pair = remote(iv, ipeer, isem.at[0], isem.at[1], at(c=1 - c))
    pair.start()

    @pl.when(owner)
    def _():
        for k in (2, 1, 3):
            scatter(0, k).start()
        for a in range(2):
            for u in range(2):
                across_owner(a, u).start()
        swap_p.start()
        for k in range(1, NX):
            scatter(0, k).wait_send()
        for k in (2, 1, 3):
            scatter(1, k).start()

    load_x.wait()
    swap_x.start()

    part = span(c * 128 + (x % 2) * SHARE, SHARE)

    def lower(parity):
        return span(c * 128 + parity * SHARE, SHARE // 2)

    def upper_of(parity):
        return span(c * 128 + parity * SHARE + SHARE // 2, SHARE // 2)

    even_x = x % 2
    lends = (lower(even_x), upper_of(even_x))
    lacks = (lower(1 - even_x), upper_of(1 - even_x))
    sides = (xp(1), xp(3))
    half = span(c * 128, 128)
    other = span((1 - c) * 128, 128)
    head_chip = (z == 0) & (y < 2)
    hcols = span(jnp.minimum(y, 1) * 128, 128)

    pair.wait_recv()
    even = jnp.full(iv.shape, c, jnp.int32) == 0
    blk[...] = jnp.concatenate(
        [jnp.where(even, iv[...], ipeer[...]), jnp.where(even, ipeer[...], iv[...])], axis=0
    ).T

    @pl.when(head_chip)
    def _():
        hv[part, hcols] = blk[part, :]

    h_y = [
        remote(hv.at[part, hcols], hv.at[part, hcols], hys.at[k - 1], hyr.at[k - 1], at(y=yp(k)))
        for k in range(1, NY)
    ]

    @pl.when(head_chip)
    def _():
        for copy in h_y:
            copy.start()

    qv[0, part, span(y * 128, 128)] = encode_chol(blk[part, :])
    mine = qv.at[0, part, span(y * 128, 128)]
    q_y = [remote(mine, mine, qys.at[k - 1], qyr.at[k - 1], at(y=yp(k))) for k in range(1, NY)]
    for copy in q_y:
        copy.start()

    @pl.when(owner_side & not_owner)
    def _():
        for s in range(2):
            scattered(s).wait_recv()
            for u in range(2):
                across(s, u).start()
        for s in range(2):
            for u in range(2):
                start_share(s, u)

    @pl.when(owner)
    def _():
        for k in range(1, NX):
            scatter(1, k).wait_send()
        for a in range(2):
            for k in (2, 1, 3):
                for u in range(2):
                    share_owner(a, k, u).start()

    @pl.when(z == 0)
    def _():
        for k in range(1, NY):
            yo = yp(NY - k)
            cols = span(jnp.minimum(yo, 1) * 128, 128)

            @pl.when(yo < 2)
            def _():
                remote(hv.at[part, cols], hv.at[part, cols], hys.at[k - 1], hyr.at[k - 1], at(y=yp(k))).wait_recv()

    h_z = [remote(hv.at[part], hv.at[part], hzs.at[k - 1], hzr.at[0], at(z=zp(k))) for k in range(1, NZ)]

    @pl.when(z == 0)
    def _():
        for k in (4, 3, 5, 2, 6, 1, 7):
            h_z[k - 1].start()

    for k in range(1, NY):
        src = qv.at[0, part, span(yp(NY - k) * 128, 128)]
        remote(src, src, qys.at[k - 1], qyr.at[k - 1], at(y=yp(k))).wait_recv()

    def block(rel, rows=part):
        return qv.at[ORDER.index(rel % NZ), rows]

    def over_z(n, k):
        return remote(block(0), block(-k), qzs.at[n], qzr.at[n], at(z=zp(k)))

    def came_over_z(n, k):
        return remote(block(-k), block(-k), qzs.at[n], qzr.at[n], at(z=zp(k)))

    def onward(n, k):
        return remote(block(-2 * k), block(-3 * k), qzs.at[4 + n], qzr.at[4 + n], at(z=zp(k)))

    def onward_half(n, k):
        rows = span(c * 128 + even_x * SHARE + n * (SHARE // 2), SHARE // 2)
        return remote(block(-2 * k, rows), block(4, rows), qzs.at[6 + n], qzr.at[6 + n], at(z=zp(2 * k)))

    first_z = ((0, 2), (1, -2), (2, 1), (3, -1))

    def came_onward(rel):
        if rel == 4:
            for n in range(2):
                rows = span(c * 128 + even_x * SHARE + n * (SHARE // 2), SHARE // 2)
                remote(block(4, rows), block(4, rows), qzs.at[6 + n], qzr.at[6 + n], at(z=zp(1))).wait_recv()
        elif rel in (3, 5):
            n = 1 if rel == 3 else 0
            remote(block(rel), block(rel), qzs.at[4 + n], qzr.at[4 + n], at(z=zp(1))).wait_recv()
        elif rel in (1, 7):
            n = 2 if rel == 7 else 3
            came_over_z(n, first_z[n][1]).wait_recv()

    def group(g, rows):
        low, high = GROUPS[g]
        return qv.at[pl.ds(low, high - low), rows]

    def over_x(g, n):
        src = group(g, lends[n])
        return remote(src, src, qxs.at[g * 2 + n], qxr.at[g * 2 + n], at(x=sides[n]))

    def start_over_x(g):
        for j in range(*GROUPS[g]):
            came_onward(ORDER[j])
        for n in range(2):
            over_x(g, n).start()

    for n, k in first_z:
        over_z(n, k).start()

    load_w.wait()
    load_k.wait()
    wpad[...] = jnp.zeros_like(wpad)
    wpad[0:ROWS, :] = wv[:, 0:PANEL_W].astype(F32)
    kpad[...] = jnp.zeros_like(kpad)
    kpad[0:64, 0:ROWS] = kv[...].astype(F32)
    ct[...] = contract(identity(PANEL_W, BF16), wpad[...].astype(BF16), 1, 1)
    col_id = lax.broadcasted_iota(jnp.int32, (PANEL_W, LANES), 0)
    group_id = lax.broadcasted_iota(jnp.int32, (PANEL_W, LANES), 1)
    repeat = jnp.where(col_id // 4 == group_id, 1.0, 0.0).astype(BF16)
    choice = contract(repeat, kpad[...].astype(BF16), 1, 0).astype(jnp.int32)
    place = col_id % 4
    drop = (
        ((place == 0) & (choice >= 3))
        | ((place == 1) & ((choice == 1) | (choice == 2) | (choice == 5)))
        | ((place == 2) & ((choice == 0) | (choice == 2) | (choice == 4)))
        | ((place == 3) & ((choice == 0) | (choice == 1) | (choice == 3)))
    )
    av[...] = jnp.where(drop, 1.0, 0.0)

    @pl.when(jnp.logical_not(owner_side))
    def _():
        for s in range(2):
            for u in range(2):
                across(s, u).wait_recv()
                start_share(s, u)

    for n, k in ((0, 1), (1, -1)):
        came_over_z(n, 2 * k).wait_recv()
        onward(n, k).start()
        onward_half(n, k).start()

    @pl.when(z > 0)
    def _():
        h_z[0].wait_recv()

    h_x = [remote(hv.at[lends[n]], hv.at[lends[n]], hxs.at[n], hxr.at[n], at(x=sides[n])) for n in range(2)]
    for copy in h_x:
        copy.start()

    def gram_part(s):
        @pl.when(not_owner)
        def _():
            for k in range(1, NX):
                for u in range(2):
                    shared(s, k, u).wait_recv()

        for tile in range(4):
            cols = slice(tile * 512, tile * 512 + 512)
            value = contract(pt[s], xv[s, :, cols], 1, 0)
            gv[tile] = value if s == 0 else gv[tile] + value

    @pl.when(owner)
    def _():
        swap_p.wait_recv()

    remote(xv.at[1 - c], xv.at[1 - c], xcs.at[1], xcr.at[1], at(c=1 - c)).wait_recv()
    gram_part(0)
    gram_part(1)

    def own_rows(zd):
        rows = span(zd * 16, 16)
        parts = [gv[tile, rows, :] for tile in range(4)]
        return [p[:, 128 * i : 128 * i + 128] for p in parts for i in range(4)]

    def place_of(tile):
        return tile if tile < 8 else tile + 1

    def pack(tiles, slot):
        most = jnp.abs(tiles[0])
        for value in tiles[1:]:
            most = jnp.maximum(most, jnp.abs(value))
        most = jnp.max(most, axis=0, keepdims=True)
        power = jnp.ceil(jnp.log2(jnp.maximum(most, 1e-30)))
        up = jnp.exp2(-power) * SUM_MAX
        for i, value in enumerate(tiles):
            msend[slot, place_of(i)] = jnp.round(value * up).astype(jnp.int32).astype(jnp.int16)
        msend[slot, 8] = jnp.broadcast_to(power, (16, 128)).astype(jnp.int32).astype(jnp.int16)

    def add(tiles, slot, low=0, high=16):
        down = jnp.exp2(mrecv[slot, 8].astype(jnp.int32).astype(F32)) * (1.0 / SUM_MAX)
        return [
            value + mrecv[slot, place_of(i)].astype(jnp.int32).astype(F32) * down if low <= i < high else value
            for i, value in enumerate(tiles)
        ]

    def message(slot_from, slot_to, k, which=None):
        src, dst = msend.at[slot_from], mrecv.at[slot_to]
        if which is not None:
            src, dst = src.at[pl.ds(8 * which, 9)], dst.at[pl.ds(8 * which, 9)]
        return remote(src, dst, rzs.at[slot_to], rzr.at[slot_to], at(z=zp(k)))

    far = [message(0, 0, 1), message(1, 1, -1), message(2, 2, 2, 0), message(2, 3, -2, 1)]
    near = [message(3, 4, 1), message(4, 5, -1)]
    second = [message(5, 6, 2), message(6, 7, -2)]
    pack(own_rows(zp(4)), 2)
    far[2].start()
    far[3].start()
    pack(own_rows(zp(3)), 0)
    far[0].start()
    pack(own_rows(zp(-3)), 1)
    far[1].start()
    pack(own_rows(zp(1)), 3)
    near[0].start()
    pack(own_rows(zp(-1)), 4)
    near[1].start()

    start_over_x(0)
    for n in range(2):
        remote(hv.at[lacks[n]], hv.at[lacks[n]], hxs.at[n], hxr.at[n], at(x=sides[n])).wait_recv()
    h_c = remote(hv.at[half], hv.at[half], hs.at[0], hr.at[0], at(c=1 - c))
    h_c.start()

    for g in range(1, len(GROUPS)):
        start_over_x(g)

    remote(hv.at[other], hv.at[other], hs.at[0], hr.at[0], at(c=1 - c)).wait_recv()
    head = hv[...]
    row_id = lax.broadcasted_iota(jnp.int32, (PANEL_W, PANEL_W), 0)
    lane_id = lax.broadcasted_iota(jnp.int32, (PANEL_W, PANEL_W), 1)
    pivot = jnp.sum(jnp.where(row_id == lane_id, head, 0.0), axis=1, keepdims=True)
    av[...] = av[...] * (1.0 / pivot)
    upper = jnp.where(lane_id > row_id, head, 0.0).T
    for b in range(PANEL_W // BLOCK):
        at_b = b * BLOCK
        dg[b, :, 0:BLOCK] = upper[at_b : at_b + BLOCK, at_b : at_b + BLOCK]

    def sweep(b, carry):
        rows = span(b * BLOCK, BLOCK)
        factor = av[rows, :]
        corner = dg[b]
        now = ct[rows, :]
        cols = [now[8 * v : 8 * v + 8, :] for v in range(BLOCK // 8)]
        for j in range(BLOCK):
            v0 = j // 8
            err = cols[v0][j % 8 : j % 8 + 1, :] * factor[j : j + 1, :]
            for v in range(v0, BLOCK // 8):
                cols[v] = cols[v] - corner[8 * v : 8 * v + 8, j : j + 1] * err
        done = jnp.concatenate(cols, axis=0)
        errors = done * factor
        et[rows, :] = errors
        update = contract(hv[rows, :], errors, 0, 0, HIGHEST)
        later = col_id >= (b + 1) * BLOCK
        ct[...] = ct[...] - jnp.where(later, update, 0.0)
        ct[rows, :] = done
        return carry

    lax.fori_loop(0, 2, sweep, 0)
    lax.fori_loop(2, 4, sweep, 0)

    for copy in far:
        copy.wait_recv()
    pack(add(add(own_rows(zp(2)), 0), 2, 0, 8), 5)
    second[0].start()
    pack(add(add(own_rows(zp(-2)), 1), 3, 8, 16), 6)
    second[1].start()

    lax.fori_loop(4, PANEL_W // BLOCK, sweep, 0)
    kept = jnp.where(drop, 0.0, ct[...]).astype(BF16)
    eye = identity(PANEL_W, BF16)
    kept_rows = contract(kept, eye, 0, 0)
    errors = et[...]
    errors_hi = errors.astype(BF16)
    errors_lo = (errors - errors_hi.astype(F32)).astype(BF16)
    eh[...] = contract(errors_hi, eye, 0, 0).astype(BF16)
    el[...] = contract(errors_lo, eye, 0, 0).astype(BF16)

    def block_z(j):
        rel = jnp.where(j % 2 == 1, (j + 1) // 2, (NZ - j // 2) % NZ)
        return lax.rem(z + rel, NZ)

    def between(g, rows):
        src = group(g, rows)
        return remote(src, src, qcs.at[g], qcr.at[g], at(c=1 - c))

    def hand_over(g):
        for n in range(2):
            src = group(g, lacks[n])
            remote(src, src, qxs.at[g * 2 + n], qxr.at[g * 2 + n], at(x=sides[n])).wait_recv()
        between(g, half).start()

    for g in range(8):
        hand_over(g)

    for copy in near + second:
        copy.wait_recv()
    tiles = own_rows(z)
    for slot in range(4, 8):
        tiles = add(tiles, slot)
    for tile in range(4):
        summed = jnp.concatenate(tiles[4 * tile : 4 * tile + 4], axis=1)
        for yd in range(NY):
            ysend[yd, tile * 4 : tile * 4 + 4, :] = summed[yd * 4 : yd * 4 + 4, :]
    r_y = [
        remote(ysend.at[yp(k)], yrecv.at[k - 1], rys.at[k - 1], ryr.at[k - 1], at(y=yp(k)))
        for k in range(1, NY)
    ]
    for copy in r_y:
        copy.start()

    def tail(j, carry):
        zb = block_z(j)
        for i in range(2):
            chol = decode_chol(qv[j, :, 256 * i : 256 * i + 256])
            chol_hi = chol.astype(BF16)
            chol_lo = (chol - chol_hi.astype(F32)).astype(BF16)
            update = contract(eh[...], chol_hi, 1, 0) + (
                contract(eh[...], chol_lo, 1, 0) + contract(el[...], chol_hi, 1, 0)
            )
            cols = span(zb * 512 + i * 256, 256)
            pruned[:, cols] = (wv[:, cols].astype(F32) - update[0:ROWS, :]).astype(BF16)
        return carry

    for g, (low, high) in enumerate(GROUPS):
        if g + 8 < len(GROUPS):
            hand_over(g + 8)
        between(g, other).wait_recv()
        lax.fori_loop(low, high, tail, 0)
    pruned[:, 0:PANEL_W] = kept_rows[0:ROWS, :].astype(BF16)

    for copy in r_y:
        copy.wait_recv()
    total = ysend[y] + yrecv[0] + yrecv[1] + yrecv[2]
    total = total * (2.0 / (TOK * NZ * NY * NC))
    for tile in range(4):
        gram[:, tile * 512 : tile * 512 + 512] = total[tile * 4 : tile * 4 + 4, :]

    @pl.when(owner)
    def _():
        swap_p.wait_send()
        for a in range(2):
            for u in range(2):
                across_owner(a, u).wait_send()
                for k in range(1, NX):
                    share_owner(a, k, u).wait_send()

    for s in range(2):
        for u in range(2):
            pl.when(owner_side & not_owner)(across(s, u).wait_send)
            for k in range(1, NX):
                pl.when(not_owner & jnp.logical_not(to_owner(k)))(share(s, k, u).wait_send)

    @pl.when(head_chip)
    def _():
        for copy in h_y:
            copy.wait_send()

    @pl.when(z == 0)
    def _():
        for copy in h_z:
            copy.wait_send()

    for copy in [pair, h_c, swap_x] + q_y + h_x + far + near + second + r_y:
        copy.wait_send()
    for n, k in first_z:
        over_z(n, k).wait_send()
    for n, k in ((0, 1), (1, -1)):
        onward(n, k).wait_send()
        onward_half(n, k).wait_send()
    for g in range(len(GROUPS)):
        for n in range(2):
            over_x(g, n).wait_send()
        between(g, half).wait_send()


def finish(pruned, gram, pruned_out, gram_out, sem):
    copies = [
        pltpu.make_async_copy(pruned, pruned_out, sem.at[0]),
        pltpu.make_async_copy(gram, gram_out, sem.at[1]),
    ]
    for copy in copies:
        copy.start()
    for copy in copies:
        copy.wait()


def shards(calib_inputs, weights, inverse_chol, keep_pattern):
    dma = pltpu.SemaphoreType.DMA
    vmem = pltpu.VMEM
    scratch = [
        vmem((NC, TOK, FEAT), BF16),
        vmem((TOK, PANEL_W), BF16),
        vmem((ROWS, WINDOW), BF16),
        vmem((64, ROWS), jnp.int32),
        vmem((64, PANEL_W), F32),
        vmem((64, PANEL_W), F32),
        vmem((PANEL_W, 128), F32),
        vmem((NZ, PANEL_W, NY * 128), jnp.int16),
        vmem((PANEL_W, PANEL_W), F32),
        vmem((4, 128, 512), F32),
        vmem((7, 17, 16, 128), jnp.int16),
        vmem((8, 17, 16, 128), jnp.int16),
        vmem((NY, 16, 512), F32),
        vmem((NY - 1, 16, 512), F32),
        vmem((LANES, PANEL_W), F32),
        vmem((LANES, LANES), F32),
        vmem((PANEL_W // BLOCK, BLOCK, 128), F32),
        vmem((PANEL_W, LANES), F32),
        vmem((PANEL_W, LANES), F32),
        vmem((PANEL_W, LANES), F32),
        vmem((LANES, PANEL_W), BF16),
        vmem((LANES, PANEL_W), BF16),
        vmem((PANEL_W, TOK), BF16),
        vmem((NC, 128, TOK), BF16),
    ]
    sems = [5, 2, 6, 2, 4, 4, 12, 12, 3, 3, 8, 8, 16, 16, 8, 8, 3, 3, 7, 1, 3, 3, 1, 1, 2, 2, 8, 8, 3, 3]
    scratch += [dma((n,)) for n in sems]
    anywhere = pl.BlockSpec(memory_space=pltpu.HBM)
    inside = pl.BlockSpec(memory_space=pltpu.VMEM)
    results = pl.pallas_call(
        kernel,
        out_shape=(
            pltpu.VMEM((ROWS, WINDOW), BF16),
            pltpu.VMEM((PANEL_W // (NZ * NY * NC), FEAT), F32),
        ),
        in_specs=[anywhere] * 4,
        out_specs=(inside, inside),
        scratch_shapes=scratch,
        compiler_params=pltpu.CompilerParams(
            collective_id=0, has_side_effects=True, vmem_limit_bytes=40 * 2**20
        ),
        cost_estimate=pl.CostEstimate(flops=2 * 10**9, bytes_accessed=8 * 10**6, transcendentals=0),
    )(*[pltpu.with_memory_space_constraint(v, pltpu.HBM) for v in (calib_inputs, weights, inverse_chol.T, keep_pattern.T)])
    return pl.pallas_call(
        finish,
        out_shape=(
            jax.ShapeDtypeStruct((ROWS, WINDOW), BF16),
            jax.ShapeDtypeStruct((PANEL_W // (NZ * NY * NC), FEAT), F32),
        ),
        in_specs=[inside, inside],
        out_specs=(anywhere, anywhere),
        scratch_shapes=[dma((2,))],
    )(*[pltpu.with_memory_space_constraint(value, pltpu.VMEM) for value in results])


def solution(mesh):
    placed = (
        P("dp", "tensor"),
        P(("dp", "tensor"), None),
        P(None, "dp"),
        P(("dp", "tensor"), None),
    )
    return jax.shard_map(
        shards,
        mesh=mesh,
        in_specs=placed,
        out_specs=(P(("dp", "tensor"), None), P("dp", "tensor")),
        check_vma=False,
    )
```

```python
import jax
import jax.numpy as jnp
from jax import lax
from jax.experimental import pallas as pl
from jax.experimental.pallas import tpu as pltpu
from jax.sharding import PartitionSpec as P

MESH = pl.DeviceIdType.MESH
NZ, NY, NC, NH, NX = 8, 4, 2, 2, 4
PANEL_W = 256
WINDOW = 4096
ROWS = 104
LANES = 128
FEAT = 2048
TOK = 768
QTOK = TOK // NX
PART = PANEL_W // (NX * NC)
SHARE = PANEL_W // (2 * NC)
OWNER_X, OWNER_H = 2, 1
BLOCK = 32
CODE_MAX = 32767.0
CHOL_MAX = 2.0
SUM_MAX = 32000.0
F32 = jnp.float32
BF16 = jnp.bfloat16
HIGHEST = lax.Precision.HIGHEST


def contract(a, b, da, db, precision=None):
    return lax.dot_general(
        a, b, (((da,), (db,)), ((), ())), precision=precision, preferred_element_type=F32
    )


def identity(n, dtype):
    rows = lax.broadcasted_iota(jnp.int32, (n, n), 0)
    cols = lax.broadcasted_iota(jnp.int32, (n, n), 1)
    return jnp.where(rows == cols, 1.0, 0.0).astype(dtype)


def panel_order():
    rows = lax.broadcasted_iota(jnp.int32, (PANEL_W, PANEL_W), 0)
    cols = lax.broadcasted_iota(jnp.int32, (PANEL_W, PANEL_W), 1)
    core, rest = rows // 128, rows % 128
    feature = (rest // 4) * 8 + core * 4 + rest % 4
    return jnp.where(feature == cols, 1.0, 0.0).astype(BF16)


def encode_chol(value):
    root = jnp.sqrt(jnp.minimum(jnp.abs(value) * (1.0 / CHOL_MAX), 1.0)) * CODE_MAX
    code = jnp.round(jnp.where(value < 0.0, -root, root))
    return code.astype(jnp.int32).astype(jnp.int16)


def decode_chol(code):
    value = code.astype(jnp.int32).astype(F32)
    return value * jnp.abs(value) * (CHOL_MAX / (CODE_MAX * CODE_MAX))


ORDER = (0, 1, 7, 2, 6, 3, 5, 4)
GROUPS = ((0, 1), (1, 2), (2, 3), (3, 4), (4, 5), (5, 6), (6, 7), (7, 8))


def kernel(
    calib, weights, inverse, pattern,
    pruned, gram,
    xv, pv, wv, kv, iv, ipeer, blk, qv, hv, gv, msend, mrecv, ysend, ypack, yrecv,
    wpad, kpad, dg, ct, av, et, eh, el, po, pt,
    lsem, isem, s1s, s1r, hcs, hcr, s2s, s2r,
    qys, qyr, qzs, qzr, qxs, qxr, qcs, qcr, hys, hyr, hzs, hzr, hxs, hxr, hs, hr,
    xcs, xcr, rzs, rzr, rys, ryr,
):
    d = lax.axis_index("dp")
    t = lax.axis_index("tensor")
    z, y, c = d // (NY * NC), (d // NC) % NY, d % NC
    h, x = t // NX, t % NX
    owner = (h == OWNER_H) & (x == OWNER_X)
    not_owner = jnp.logical_not(owner)
    owner_side = h == OWNER_H

    def at(z=z, y=y, c=c, h=h, x=x):
        return ((z * NY + y) * NC + c, h * NX + x)

    def remote(src, dst, send, recv, where):
        return pltpu.make_async_remote_copy(
            src_ref=src, dst_ref=dst, send_sem=send, recv_sem=recv,
            device_id=where, device_id_type=MESH,
        )

    def zp(k):
        return lax.rem(z + k + NZ, NZ)

    def yp(k):
        return lax.rem(y + k, NY)

    def xp(k):
        return lax.rem(x + k, NX)

    def span(start, size):
        return pl.ds(pl.multiple_of(start, size), size)

    load_i = pltpu.make_async_copy(inverse, iv, lsem.at[0])
    load_x = pltpu.make_async_copy(calib, xv.at[c], lsem.at[1])
    load_w = pltpu.make_async_copy(weights, wv, lsem.at[2])
    load_k = pltpu.make_async_copy(pattern, kv, lsem.at[3])
    load_p = pltpu.make_async_copy(calib.at[:, pl.ds(0, PANEL_W)], pv, lsem.at[4])
    pl.when(owner)(load_p.start)
    load_i.start()
    load_x.start()
    load_w.start()
    load_k.start()

    barrier = pltpu.get_barrier_semaphore()
    partners = [at(x=xp(k), c=c) for k in range(1, NX)] + [at(x=xp(k), c=1 - c) for k in range(1, NX)]
    partners += [at(h=1 - h), at(h=1 - h, c=1 - c), at(c=1 - c)]
    partners += [at(y=yp(k)) for k in range(1, NY)]
    partners += [at(z=zp(k)) for k in range(1, NZ)]
    for partner in partners:
        pl.semaphore_signal(barrier, inc=1, device_id=partner, device_id_type=MESH)

    @pl.when(owner)
    def _():
        load_p.wait()
        po[...] = contract(panel_order(), pv[...], 1, 1).astype(BF16)
        pt[c] = po[span(c * 128, 128), :]

    load_i.wait()
    pl.semaphore_wait(barrier, len(partners))

    def ordered(a, xo):
        return po.at[span(a * 128 + xo * PART, PART)]

    def piece(s, xo):
        return pt.at[s, span(xo * PART, PART)]

    def scatter(a, k):
        return remote(ordered(a, xp(k)), piece(c, xp(k)), s1s.at[a * 3 + k - 1], s1r.at[c], at(x=xp(k), c=a))

    def scattered(s):
        return remote(piece(s, x), piece(s, x), s1s.at[s], s1r.at[s], at(x=xp(1)))

    def across_owner(a, u):
        src = po.at[span(a * 128 + x * PART + u * 16, 16)]
        return remote(src, sub(c, x, u), hcs.at[a * 2 + u], hcr.at[c * 2 + u], at(h=1 - h, c=a))

    def sub(s, xo, u):
        return pt.at[s, span(xo * PART + u * 16, 16)]

    def across(s, u):
        sem = s * 2 + u
        return remote(sub(s, x, u), sub(s, x, u), hcs.at[sem], hcr.at[sem], at(h=1 - h))

    def share_owner(a, k, u):
        src = po.at[span(a * 128 + x * PART + u * 16, 16)]
        sem = s2r.at[(c * 3 + k - 1) * 2 + u]
        return remote(src, sub(c, x, u), s2s.at[(a * 3 + k - 1) * 2 + u], sem, at(x=xp(k), c=a))

    def share(s, k, u):
        sem = (s * 3 + k - 1) * 2 + u
        return remote(sub(s, x, u), sub(s, x, u), s2s.at[sem], s2r.at[sem], at(x=xp(k)))

    def shared(s, k, u):
        src = sub(s, xp(NX - k), u)
        sem = (s * 3 + k - 1) * 2 + u
        return remote(src, src, s2s.at[sem], s2r.at[sem], at(x=xp(k)))

    swap_p = remote(po.at[span((1 - c) * 128, 128)], pt.at[c], xcs.at[0], xcr.at[0], at(c=1 - c))
    swap_x = remote(xv.at[c], xv.at[c], xcs.at[1], xcr.at[1], at(c=1 - c))

    def to_owner(k):
        return owner_side & (xp(k) == OWNER_X)

    def start_share(s, u):
        for k in (2, 1, 3):
            pl.when(jnp.logical_not(to_owner(k)))(share(s, k, u).start)

    pair = remote(iv, ipeer, isem.at[0], isem.at[1], at(c=1 - c))
    pair.start()

    @pl.when(owner)
    def _():
        for k in (2, 1, 3):
            scatter(0, k).start()
        for a in range(2):
            for u in range(2):
                across_owner(a, u).start()
        swap_p.start()
        for k in range(1, NX):
            scatter(0, k).wait_send()
        for k in (2, 1, 3):
            scatter(1, k).start()

    load_x.wait()
    swap_x.start()

    part = span(c * 128 + (x % 2) * SHARE, SHARE)

    def lower(parity):
        return span(c * 128 + parity * SHARE, SHARE // 2)

    def upper_of(parity):
        return span(c * 128 + parity * SHARE + SHARE // 2, SHARE // 2)

    even_x = x % 2
    lends = (lower(even_x), upper_of(even_x))
    lacks = (lower(1 - even_x), upper_of(1 - even_x))
    sides = (xp(1), xp(3))
    half = span(c * 128, 128)
    other = span((1 - c) * 128, 128)
    head_chip = (z == 0) & (y < 2)
    hcols = span(jnp.minimum(y, 1) * 128, 128)

    pair.wait_recv()
    even = jnp.full(iv.shape, c, jnp.int32) == 0
    blk[...] = jnp.concatenate(
        [jnp.where(even, iv[...], ipeer[...]), jnp.where(even, ipeer[...], iv[...])], axis=0
    ).T

    @pl.when(head_chip)
    def _():
        hv[part, hcols] = blk[part, :]

    h_y = [
        remote(hv.at[part, hcols], hv.at[part, hcols], hys.at[k - 1], hyr.at[k - 1], at(y=yp(k)))
        for k in range(1, NY)
    ]

    @pl.when(head_chip)
    def _():
        for copy in h_y:
            copy.start()

    qv[0, part, span(y * 128, 128)] = encode_chol(blk[part, :])
    mine = qv.at[0, part, span(y * 128, 128)]
    q_y = [remote(mine, mine, qys.at[k - 1], qyr.at[k - 1], at(y=yp(k))) for k in range(1, NY)]
    for copy in q_y:
        copy.start()

    @pl.when(owner_side & not_owner)
    def _():
        for s in range(2):
            scattered(s).wait_recv()
            for u in range(2):
                across(s, u).start()
        for s in range(2):
            for u in range(2):
                start_share(s, u)

    @pl.when(owner)
    def _():
        for k in range(1, NX):
            scatter(1, k).wait_send()
        for a in range(2):
            for k in (2, 1, 3):
                for u in range(2):
                    share_owner(a, k, u).start()

    @pl.when(z == 0)
    def _():
        for k in range(1, NY):
            yo = yp(NY - k)
            cols = span(jnp.minimum(yo, 1) * 128, 128)

            @pl.when(yo < 2)
            def _():
                remote(hv.at[part, cols], hv.at[part, cols], hys.at[k - 1], hyr.at[k - 1], at(y=yp(k))).wait_recv()

    h_z = [remote(hv.at[part], hv.at[part], hzs.at[k - 1], hzr.at[0], at(z=zp(k))) for k in range(1, NZ)]

    @pl.when(z == 0)
    def _():
        for k in (4, 3, 5, 2, 6, 1, 7):
            h_z[k - 1].start()

    for k in range(1, NY):
        src = qv.at[0, part, span(yp(NY - k) * 128, 128)]
        remote(src, src, qys.at[k - 1], qyr.at[k - 1], at(y=yp(k))).wait_recv()

    def block(rel, rows=part):
        return qv.at[ORDER.index(rel % NZ), rows]

    def over_z(n, k):
        return remote(block(0), block(-k), qzs.at[n], qzr.at[n], at(z=zp(k)))

    def came_over_z(n, k):
        return remote(block(-k), block(-k), qzs.at[n], qzr.at[n], at(z=zp(k)))

    def onward(n, k):
        return remote(block(-2 * k), block(-3 * k), qzs.at[4 + n], qzr.at[4 + n], at(z=zp(k)))

    def onward_half(n, k):
        rows = span(c * 128 + even_x * SHARE + n * (SHARE // 2), SHARE // 2)
        return remote(block(-2 * k, rows), block(4, rows), qzs.at[6 + n], qzr.at[6 + n], at(z=zp(2 * k)))

    first_z = ((0, 2), (1, -2), (2, 1), (3, -1))

    def came_onward(rel):
        if rel == 4:
            for n in range(2):
                rows = span(c * 128 + even_x * SHARE + n * (SHARE // 2), SHARE // 2)
                remote(block(4, rows), block(4, rows), qzs.at[6 + n], qzr.at[6 + n], at(z=zp(1))).wait_recv()
        elif rel in (3, 5):
            n = 1 if rel == 3 else 0
            remote(block(rel), block(rel), qzs.at[4 + n], qzr.at[4 + n], at(z=zp(1))).wait_recv()
        elif rel in (1, 7):
            n = 2 if rel == 7 else 3
            came_over_z(n, first_z[n][1]).wait_recv()

    def group(g, rows):
        low, high = GROUPS[g]
        return qv.at[pl.ds(low, high - low), rows]

    def over_x(g, n):
        src = group(g, lends[n])
        return remote(src, src, qxs.at[g * 2 + n], qxr.at[g * 2 + n], at(x=sides[n]))

    def start_over_x(g):
        for j in range(*GROUPS[g]):
            came_onward(ORDER[j])
        for n in range(2):
            over_x(g, n).start()

    for n, k in first_z:
        over_z(n, k).start()

    load_w.wait()
    load_k.wait()
    wpad[...] = jnp.zeros_like(wpad)
    wpad[0:ROWS, :] = wv[:, 0:PANEL_W].astype(F32)
    kpad[...] = jnp.zeros_like(kpad)
    kpad[0:64, 0:ROWS] = kv[...].astype(F32)
    ct[...] = contract(identity(PANEL_W, BF16), wpad[...].astype(BF16), 1, 1)
    col_id = lax.broadcasted_iota(jnp.int32, (PANEL_W, LANES), 0)
    group_id = lax.broadcasted_iota(jnp.int32, (PANEL_W, LANES), 1)
    repeat = jnp.where(col_id // 4 == group_id, 1.0, 0.0).astype(BF16)
    choice = contract(repeat, kpad[...].astype(BF16), 1, 0).astype(jnp.int32)
    place = col_id % 4
    drop = (
        ((place == 0) & (choice >= 3))
        | ((place == 1) & ((choice == 1) | (choice == 2) | (choice == 5)))
        | ((place == 2) & ((choice == 0) | (choice == 2) | (choice == 4)))
        | ((place == 3) & ((choice == 0) | (choice == 1) | (choice == 3)))
    )
    av[...] = jnp.where(drop, 1.0, 0.0)

    @pl.when(jnp.logical_not(owner_side))
    def _():
        for s in range(2):
            for u in range(2):
                across(s, u).wait_recv()
                start_share(s, u)

    for n, k in ((0, 1), (1, -1)):
        came_over_z(n, 2 * k).wait_recv()
        onward(n, k).start()
        onward_half(n, k).start()

    @pl.when(z > 0)
    def _():
        h_z[0].wait_recv()

    h_x = [remote(hv.at[lends[n]], hv.at[lends[n]], hxs.at[n], hxr.at[n], at(x=sides[n])) for n in range(2)]
    for copy in h_x:
        copy.start()

    def gram_part(s):
        @pl.when(not_owner)
        def _():
            for k in range(1, NX):
                for u in range(2):
                    shared(s, k, u).wait_recv()

        for tile in range(4):
            cols = slice(tile * 512, tile * 512 + 512)
            value = contract(pt[s], xv[s, :, cols], 1, 0)
            gv[tile] = value if s == 0 else gv[tile] + value

    @pl.when(owner)
    def _():
        swap_p.wait_recv()

    remote(xv.at[1 - c], xv.at[1 - c], xcs.at[1], xcr.at[1], at(c=1 - c)).wait_recv()
    gram_part(0)
    gram_part(1)

    def own_rows(zd):
        rows = span(zd * 16, 16)
        parts = [gv[tile, rows, :] for tile in range(4)]
        return [p[:, 128 * i : 128 * i + 128] for p in parts for i in range(4)]

    def place_of(tile):
        return tile if tile < 8 else tile + 1

    def pack(tiles, slot):
        most = jnp.abs(tiles[0])
        for value in tiles[1:]:
            most = jnp.maximum(most, jnp.abs(value))
        most = jnp.max(most, axis=0, keepdims=True)
        power = jnp.ceil(jnp.log2(jnp.maximum(most, 1e-30)))
        up = jnp.exp2(-power) * SUM_MAX
        for i, value in enumerate(tiles):
            msend[slot, place_of(i)] = jnp.round(value * up).astype(jnp.int32).astype(jnp.int16)
        msend[slot, 8] = jnp.broadcast_to(power, (16, 128)).astype(jnp.int32).astype(jnp.int16)

    def add(tiles, slot, low=0, high=16):
        down = jnp.exp2(mrecv[slot, 8].astype(jnp.int32).astype(F32)) * (1.0 / SUM_MAX)
        return [
            value + mrecv[slot, place_of(i)].astype(jnp.int32).astype(F32) * down if low <= i < high else value
            for i, value in enumerate(tiles)
        ]

    def message(slot_from, slot_to, k, which=None):
        src, dst = msend.at[slot_from], mrecv.at[slot_to]
        if which is not None:
            src, dst = src.at[pl.ds(8 * which, 9)], dst.at[pl.ds(8 * which, 9)]
        return remote(src, dst, rzs.at[slot_to], rzr.at[slot_to], at(z=zp(k)))

    far = [message(0, 0, 1), message(1, 1, -1), message(2, 2, 2, 0), message(2, 3, -2, 1)]
    near = [message(3, 4, 1), message(4, 5, -1)]
    second = [message(5, 6, 2), message(6, 7, -2)]
    pack(own_rows(zp(4)), 2)
    far[2].start()
    far[3].start()
    pack(own_rows(zp(3)), 0)
    far[0].start()
    pack(own_rows(zp(-3)), 1)
    far[1].start()
    pack(own_rows(zp(1)), 3)
    near[0].start()
    pack(own_rows(zp(-1)), 4)
    near[1].start()

    start_over_x(0)
    for n in range(2):
        remote(hv.at[lacks[n]], hv.at[lacks[n]], hxs.at[n], hxr.at[n], at(x=sides[n])).wait_recv()
    h_c = remote(hv.at[half], hv.at[half], hs.at[0], hr.at[0], at(c=1 - c))
    h_c.start()

    for g in range(1, len(GROUPS)):
        start_over_x(g)

    remote(hv.at[other], hv.at[other], hs.at[0], hr.at[0], at(c=1 - c)).wait_recv()
    head = hv[...]
    row_id = lax.broadcasted_iota(jnp.int32, (PANEL_W, PANEL_W), 0)
    lane_id = lax.broadcasted_iota(jnp.int32, (PANEL_W, PANEL_W), 1)
    pivot = jnp.sum(jnp.where(row_id == lane_id, head, 0.0), axis=1, keepdims=True)
    av[...] = av[...] * (1.0 / pivot)
    upper = jnp.where(lane_id > row_id, head, 0.0).T
    for b in range(PANEL_W // BLOCK):
        at_b = b * BLOCK
        dg[b, :, 0:BLOCK] = upper[at_b : at_b + BLOCK, at_b : at_b + BLOCK]

    def sweep(b, carry):
        rows = span(b * BLOCK, BLOCK)
        factor = av[rows, :]
        corner = dg[b]
        now = ct[rows, :]
        cols = [now[8 * v : 8 * v + 8, :] for v in range(BLOCK // 8)]
        for j in range(BLOCK):
            v0 = j // 8
            err = cols[v0][j % 8 : j % 8 + 1, :] * factor[j : j + 1, :]
            for v in range(v0, BLOCK // 8):
                cols[v] = cols[v] - corner[8 * v : 8 * v + 8, j : j + 1] * err
        done = jnp.concatenate(cols, axis=0)
        errors = done * factor
        et[rows, :] = errors
        update = contract(hv[rows, :], errors, 0, 0, HIGHEST)
        later = col_id >= (b + 1) * BLOCK
        ct[...] = ct[...] - jnp.where(later, update, 0.0)
        ct[rows, :] = done
        return carry

    lax.fori_loop(0, 2, sweep, 0)
    lax.fori_loop(2, 4, sweep, 0)

    for copy in far:
        copy.wait_recv()
    pack(add(add(own_rows(zp(2)), 0), 2, 0, 8), 5)
    second[0].start()
    pack(add(add(own_rows(zp(-2)), 1), 3, 8, 16), 6)
    second[1].start()

    lax.fori_loop(4, PANEL_W // BLOCK, sweep, 0)
    kept = jnp.where(drop, 0.0, ct[...]).astype(BF16)
    eye = identity(PANEL_W, BF16)
    kept_rows = contract(kept, eye, 0, 0)
    errors = et[...]
    errors_hi = errors.astype(BF16)
    errors_lo = (errors - errors_hi.astype(F32)).astype(BF16)
    eh[...] = contract(errors_hi, eye, 0, 0).astype(BF16)
    el[...] = contract(errors_lo, eye, 0, 0).astype(BF16)

    def block_z(j):
        rel = jnp.where(j % 2 == 1, (j + 1) // 2, (NZ - j // 2) % NZ)
        return lax.rem(z + rel, NZ)

    def between(g, rows):
        src = group(g, rows)
        return remote(src, src, qcs.at[g], qcr.at[g], at(c=1 - c))

    def hand_over(g):
        for n in range(2):
            src = group(g, lacks[n])
            remote(src, src, qxs.at[g * 2 + n], qxr.at[g * 2 + n], at(x=sides[n])).wait_recv()
        between(g, half).start()

    for g in range(8):
        hand_over(g)

    for copy in near + second:
        copy.wait_recv()
    tiles = own_rows(z)
    for slot in range(4, 8):
        tiles = add(tiles, slot)
    for tile in range(4):
        summed = jnp.concatenate(tiles[4 * tile : 4 * tile + 4], axis=1)
        for yd in range(NY):
            ysend[yd, tile * 4 : tile * 4 + 4, :] = summed[yd * 4 : yd * 4 + 4, :]
    for yd in range(NY):
        value = ysend[yd]
        most = jnp.abs(value[:, 0:128])
        for i in range(1, 4):
            most = jnp.maximum(most, jnp.abs(value[:, 128 * i : 128 * i + 128]))
        most = jnp.max(most, axis=0, keepdims=True)
        power = jnp.ceil(jnp.log2(jnp.maximum(most, 1e-30)))
        up = jnp.exp2(-power) * SUM_MAX
        for i in range(4):
            code = jnp.round(value[:, 128 * i : 128 * i + 128] * up)
            ypack[yd, i] = code.astype(jnp.int32).astype(jnp.int16)
        ypack[yd, 4] = jnp.broadcast_to(power, (16, 128)).astype(jnp.int32).astype(jnp.int16)
    r_y = [
        remote(ypack.at[yp(k)], yrecv.at[k - 1], rys.at[k - 1], ryr.at[k - 1], at(y=yp(k)))
        for k in range(1, NY)
    ]
    for copy in r_y:
        copy.start()

    def tail(j, carry):
        zb = block_z(j)
        for i in range(2):
            chol = decode_chol(qv[j, :, 256 * i : 256 * i + 256])
            chol_hi = chol.astype(BF16)
            chol_lo = (chol - chol_hi.astype(F32)).astype(BF16)
            update = contract(eh[...], chol_hi, 1, 0) + (
                contract(eh[...], chol_lo, 1, 0) + contract(el[...], chol_hi, 1, 0)
            )
            cols = span(zb * 512 + i * 256, 256)
            pruned[:, cols] = (wv[:, cols].astype(F32) - update[0:ROWS, :]).astype(BF16)
        return carry

    for g, (low, high) in enumerate(GROUPS):
        if g + 8 < len(GROUPS):
            hand_over(g + 8)
        between(g, other).wait_recv()
        lax.fori_loop(low, high, tail, 0)
    pruned[:, 0:PANEL_W] = kept_rows[0:ROWS, :].astype(BF16)

    for copy in r_y:
        copy.wait_recv()
    total = ysend[y]
    for k in range(NY - 1):
        down = jnp.exp2(yrecv[k, 4].astype(jnp.int32).astype(F32)) * (1.0 / SUM_MAX)
        total = total + jnp.concatenate(
            [yrecv[k, i].astype(jnp.int32).astype(F32) * down for i in range(4)], axis=1
        )
    total = total * (2.0 / (TOK * NZ * NY * NC))
    for tile in range(4):
        gram[:, tile * 512 : tile * 512 + 512] = total[tile * 4 : tile * 4 + 4, :]

    @pl.when(owner)
    def _():
        swap_p.wait_send()
        for a in range(2):
            for u in range(2):
                across_owner(a, u).wait_send()
                for k in range(1, NX):
                    share_owner(a, k, u).wait_send()

    for s in range(2):
        for u in range(2):
            pl.when(owner_side & not_owner)(across(s, u).wait_send)
            for k in range(1, NX):
                pl.when(not_owner & jnp.logical_not(to_owner(k)))(share(s, k, u).wait_send)

    @pl.when(head_chip)
    def _():
        for copy in h_y:
            copy.wait_send()

    @pl.when(z == 0)
    def _():
        for copy in h_z:
            copy.wait_send()

    for copy in [pair, h_c, swap_x] + q_y + h_x + far + near + second + r_y:
        copy.wait_send()
    for n, k in first_z:
        over_z(n, k).wait_send()
    for n, k in ((0, 1), (1, -1)):
        onward(n, k).wait_send()
        onward_half(n, k).wait_send()
    for g in range(len(GROUPS)):
        for n in range(2):
            over_x(g, n).wait_send()
        between(g, half).wait_send()


def finish(pruned, gram, pruned_out, gram_out, sem):
    copies = [
        pltpu.make_async_copy(pruned, pruned_out, sem.at[0]),
        pltpu.make_async_copy(gram, gram_out, sem.at[1]),
    ]
    for copy in copies:
        copy.start()
    for copy in copies:
        copy.wait()


def shards(calib_inputs, weights, inverse_chol, keep_pattern):
    dma = pltpu.SemaphoreType.DMA
    vmem = pltpu.VMEM
    scratch = [
        vmem((NC, TOK, FEAT), BF16),
        vmem((TOK, PANEL_W), BF16),
        vmem((ROWS, WINDOW), BF16),
        vmem((64, ROWS), jnp.int32),
        vmem((64, PANEL_W), F32),
        vmem((64, PANEL_W), F32),
        vmem((PANEL_W, 128), F32),
        vmem((NZ, PANEL_W, NY * 128), jnp.int16),
        vmem((PANEL_W, PANEL_W), F32),
        vmem((4, 128, 512), F32),
        vmem((7, 17, 16, 128), jnp.int16),
        vmem((8, 17, 16, 128), jnp.int16),
        vmem((NY, 16, 512), F32),
        vmem((NY, 5, 16, 128), jnp.int16),
        vmem((NY - 1, 5, 16, 128), jnp.int16),
        vmem((LANES, PANEL_W), F32),
        vmem((LANES, LANES), F32),
        vmem((PANEL_W // BLOCK, BLOCK, 128), F32),
        vmem((PANEL_W, LANES), F32),
        vmem((PANEL_W, LANES), F32),
        vmem((PANEL_W, LANES), F32),
        vmem((LANES, PANEL_W), BF16),
        vmem((LANES, PANEL_W), BF16),
        vmem((PANEL_W, TOK), BF16),
        vmem((NC, 128, TOK), BF16),
    ]
    sems = [5, 2, 6, 2, 4, 4, 12, 12, 3, 3, 8, 8, 16, 16, 8, 8, 3, 3, 7, 1, 3, 3, 1, 1, 2, 2, 8, 8, 3, 3]
    scratch += [dma((n,)) for n in sems]
    anywhere = pl.BlockSpec(memory_space=pltpu.HBM)
    inside = pl.BlockSpec(memory_space=pltpu.VMEM)
    results = pl.pallas_call(
        kernel,
        out_shape=(
            pltpu.VMEM((ROWS, WINDOW), BF16),
            pltpu.VMEM((PANEL_W // (NZ * NY * NC), FEAT), F32),
        ),
        in_specs=[anywhere] * 4,
        out_specs=(inside, inside),
        scratch_shapes=scratch,
        compiler_params=pltpu.CompilerParams(
            collective_id=0, has_side_effects=True, vmem_limit_bytes=40 * 2**20
        ),
        cost_estimate=pl.CostEstimate(flops=2 * 10**9, bytes_accessed=8 * 10**6, transcendentals=0),
    )(*[pltpu.with_memory_space_constraint(v, pltpu.HBM) for v in (calib_inputs, weights, inverse_chol.T, keep_pattern.T)])
    return pl.pallas_call(
        finish,
        out_shape=(
            jax.ShapeDtypeStruct((ROWS, WINDOW), BF16),
            jax.ShapeDtypeStruct((PANEL_W // (NZ * NY * NC), FEAT), F32),
        ),
        in_specs=[inside, inside],
        out_specs=(anywhere, anywhere),
        scratch_shapes=[dma((2,))],
    )(*[pltpu.with_memory_space_constraint(value, pltpu.VMEM) for value in results])


def solution(mesh):
    placed = (
        P("dp", "tensor"),
        P(("dp", "tensor"), None),
        P(None, "dp"),
        P(("dp", "tensor"), None),
    )
    return jax.shard_map(
        shards,
        mesh=mesh,
        in_specs=placed,
        out_specs=(P(("dp", "tensor"), None), P("dp", "tensor")),
        check_vma=False,
    )
```
